128 devices in a mesh: aa: 16 (over y, x_hi, core), ba: 8 (over x_lo, z).
Axes of the slice: x: 4 (x_hi: 2, x_lo: 2; x = x_hi * 2 + x_lo), y: 4, z: 4, core: 2. Of those that a mesh axis runs over, the one named last changes fastest.
Arguments:
- features: bfloat16 [65536, 128], P(('aa', 'ba')), may hold values from -6 to 6
- tile_values: bfloat16 [16384, 128, 128], P(('aa', 'ba')), may hold values from -0.125 to 0.125
- tile_row: int32 [16384], P(('aa', 'ba')), may hold values from -1 to 511, as said below
- tile_col: int32 [16384], P(('aa', 'ba')), may hold values from -1 to 511, as said below
- weight_one: bfloat16 [128, 1024], replicated, may hold values from -0.5 to 0.5
- bias_one: float32 [1024], replicated, may hold values from -3 to 3
- weight_two: bfloat16 [1024, 1024], replicated, may hold values from -0.1875 to 0.1875
Outputs:
- layer_two: bfloat16 [65536, 1024], P('aa', 'ba')
The draws below stay inside these ranges and needn't reach their ends.
Inputs may be any that keep to these rules, and one draw needn't show every extreme that they name: Slot s belongs to device s // 128, devices in the order of aa then ba. A live slot of device (a, b) names a row block from a * 32 to a * 32 + 31; an empty slot holds -1 in tile_row and in tile_col. A device's live slots come first among its slots; some device has all 128 slots live. Tiles may repeat. `tile_col`: A live slot of device (a, b) names a column block c with (c // 4) % (number of ba devices) == b.
All inputs are finite; a program needn't handle non-finite values.
Results may differ from the reference program's by a relative error of at most 0.0063.
Values may be sent and summed in bfloat16 or wider, within the bound.
A program may use at most 192 MiB of HBM per device.

```python
import jax
import jax.numpy as jnp
from jax import lax

TILE = 128
F = 128
HID = 1024
NBD = 4
CAP = 128
NBA = 32
NB = 512
ROWS = 65536
SLOTS = 16384
N_AA = 16
N_BA = 8


def tile_pattern(key):
    device_count = N_AA * N_BA
    slot_count = CAP * device_count
    live_counts = jax.random.randint(jax.random.fold_in(key, 11), (device_count,), CAP // 8, CAP + 1)
    special = jax.random.randint(jax.random.fold_in(key, 12), (), 0, device_count)
    live_counts = jnp.where(jnp.arange(device_count) == special, CAP, live_counts)
    slot_ids = jnp.arange(slot_count)
    owner = slot_ids // CAP
    owner_aa = owner // N_BA
    owner_ba = owner % N_BA
    live = slot_ids % CAP < live_counts[owner]
    row_ids = owner_aa * NBA + jax.random.randint(jax.random.fold_in(key, 13), (slot_count,), 0, NBA)
    source_aa = jax.random.randint(jax.random.fold_in(key, 14), (slot_count,), 0, N_AA)
    within = jax.random.randint(jax.random.fold_in(key, 15), (slot_count,), 0, NBD)
    col_ids = (source_aa * N_BA + owner_ba) * NBD + within
    return (jnp.where(live, row_ids, -1).astype(jnp.int32), jnp.where(live, col_ids, -1).astype(jnp.int32))


def draw_tile_row(key, part):
    row_ids, col_ids = tile_pattern(key)
    return row_ids


def draw_tile_col(key, part):
    row_ids, col_ids = tile_pattern(key)
    return col_ids


def block_levels(key, shape, cuts, least, largest):
    def one(position, parts):
        draws = jax.random.uniform(jax.random.fold_in(jax.random.fold_in(key, 6), position), (parts,), jnp.float32, least / len(cuts), largest / len(cuts))
        return jnp.repeat(jnp.exp(draws), shape[position] // parts).reshape((-1,) + (1,) * (len(shape) - position - 1))

    level = one(*cuts[0])
    for cut in cuts[1:]:
        level = level * one(*cut)
    return level


def normal_values(key, extent, deviation, most, cuts=(), dtype=jnp.bfloat16):
    level = block_levels(key, extent, cuts, -0.22, 0.18) if cuts else 1.0
    drawn = jax.random.normal(key, extent, jnp.float32) * deviation * level
    return jnp.minimum(jnp.maximum(drawn, -most), most).astype(dtype)


def setup_inputs(seed: int = 0) -> dict:
    splits = jax.random.split(jax.random.key(seed), 8)
    return {
        "features": normal_values(splits[0], (ROWS, F), 1.0, 6.0, ((0, 128),)),
        "tile_values": normal_values(splits[1], (SLOTS, TILE, TILE), (TILE * CAP // (2 * NBD)) ** -0.5, 0.125, ((0, 128),)),
        "tile_row": draw_tile_row(jax.random.fold_in(splits[7], 71), 0),
        "tile_col": draw_tile_col(jax.random.fold_in(splits[7], 71), 0),
        "weight_one": normal_values(splits[4], (F, HID), F ** -0.5, 0.5),
        "bias_one": normal_values(splits[5], (HID,), 0.5, 3.0, (), jnp.float32),
        "weight_two": normal_values(splits[6], (HID, HID), HID ** -0.5, 0.1875),
    }


def aggregate(source, tile_values, tile_row, tile_col):
    feat_width = source.shape[1]
    source_blocks = source.reshape(NB, TILE, feat_width)

    def one_turn(running, pieces):
        tile_vals, row_ids, col_ids = pieces
        picked = source_blocks[jnp.maximum(col_ids, 0)]
        products = jnp.einsum("sab,sbf->saf", tile_vals.astype(jnp.float32), picked.astype(jnp.float32), precision=lax.Precision.HIGHEST)
        target = jnp.where(row_ids < 0, NB, row_ids).astype(jnp.int32)
        return running.at[target].add(products), None

    start_sum = jnp.zeros((NB + 1, TILE, feat_width), jnp.float32)
    turn_count = N_AA * N_BA
    running, _ = lax.scan(one_turn, start_sum, (tile_values.reshape(turn_count, CAP, TILE, TILE), tile_row.reshape(turn_count, CAP), tile_col.reshape(turn_count, CAP)))
    return running[:NB].reshape(NB * TILE, feat_width)


def reference(features, tile_values, tile_row, tile_col, weight_one, bias_one, weight_two):
    aggregated = aggregate(features, tile_values, tile_row, tile_col)
    aggregated_low = aggregated.astype(jnp.bfloat16)
    hidden = jax.nn.relu(jnp.dot(aggregated_low, weight_one, preferred_element_type=jnp.float32) + bias_one).astype(jnp.bfloat16)
    projected = jnp.dot(hidden, weight_two, preferred_element_type=jnp.float32).astype(jnp.bfloat16)
    return aggregate(projected, tile_values, tile_row, tile_col).astype(jnp.bfloat16)
```

```python
import functools

import jax
import jax.numpy as jnp
from jax import lax
from jax.experimental import pallas as pl
from jax.experimental.pallas import tpu as pltpu
from jax.sharding import PartitionSpec as P

MESH = pl.DeviceIdType.MESH
TILE = 128
NZ = 4
NB = 8
NA = 16
RB = 32
N1 = 18
H1 = N1 // 2
N2 = RB - N1
H2 = N2 // 2
M0P, M0M, M1P, M1M, M2P, M2M = 0, N1, 2 * N1, 3 * N1, 4 * N1, 5 * N1
XS = 6 * N1
T2 = XS + 4 * N2
T1 = T2 + N2
T3 = T1 + N2
XF = T3 + N2
BLOCKS = XF + N1
PAIRS = 80
BF = jnp.bfloat16
F32 = jnp.float32
CT = jnp.float32


def prepare(tile_row, tile_col):
    slots = tile_row.shape[0]
    row = jnp.where(tile_row < 0, -1, tile_row % RB)
    clamped = jnp.maximum(tile_col, 0)
    col = clamped // (4 * NB) * 4 + clamped % 4
    blocks = jnp.arange(RB, dtype=jnp.int32)
    ids = jnp.arange(slots, dtype=jnp.int32)
    hot = row[:, None] == blocks[None, :]
    count = jnp.sum(hot, axis=0, dtype=jnp.int32)
    pairs = (count + 1) // 2
    start = jnp.sum(jnp.where(blocks[None, :] < blocks[:, None], pairs[None, :], 0), axis=1)
    rank = jnp.sum((row[:, None] == row[None, :]) & (ids[None, :] < ids[:, None]), axis=1, dtype=jnp.int32)
    place = jnp.where(row >= 0, 2 * jnp.sum(jnp.where(hot, start[None, :], 0), axis=1) + rank, -1)
    positions = jnp.arange(2 * PAIRS, dtype=jnp.int32)
    match = place[None, :] == positions[:, None]
    slot_at = slots + jnp.sum(jnp.where(match, ids[None, :] - slots, 0), axis=1)
    col_at = jnp.sum(jnp.where(match, col[None, :], 0), axis=1)
    q = jnp.arange(PAIRS, dtype=jnp.int32)
    inside = (q[:, None] > start[None, :]) & (q[:, None] < (start + pairs)[None, :])
    keep = jnp.sum(inside, axis=1).astype(F32)
    last = jnp.where(count > 0, start + pairs - 1, PAIRS)
    return slot_at, col_at, keep, last


def kernel(
    slot_at, col_at, keep, last, x_ref, tiles_hbm, w1_ref, b1_ref, w2_hbm, out_ref,
    tiles, w2c, feats, send_c, recv_c, lows, sb, rb,
    loc_sem, as_sem, ar_sem, fs_sem, fr_sem, cs_sem, cr_sem, ds_sem, dr_sem, gs_sem, gr_sem, es_sem, er_sem,
):
    a, b = lax.axis_index("aa"), lax.axis_index("ba")
    y, xh, c = a // 4, lax.rem(a // 2, 2), lax.rem(a, 2)
    xl, z = b // NZ, lax.rem(b, NZ)

    def aa_of(dy, dx):
        return lax.rem(y + dy, 4) * 4 + lax.rem(xh + dx, 2) * 2 + c

    def ba_of(dx, dz):
        return lax.rem(xl + dx, 2) * NZ + lax.rem(z + dz, NZ)

    sibling = (a + 1 - 2 * c, b)

    tile_copy = pltpu.make_async_copy(tiles_hbm, tiles.at[pl.ds(0, 128)], loc_sem.at[0])
    tile_copy.start()
    w2_copies = []
    for f in range(NB):
        w2_copies.append(
            pltpu.make_async_copy(
                w2_hbm.at[:, pl.ds(f * TILE, TILE)],
                w2c.at[f],
                loc_sem.at[1 + f],
            )
        )
        w2_copies[-1].start()

    barrier = pltpu.get_barrier_semaphore()
    for k in range(1, 8):
        pl.semaphore_signal(barrier, inc=1, device_id=(aa_of(k // 2, k % 2), b), device_id_type=MESH)
        pl.semaphore_signal(barrier, inc=1, device_id=(a, ba_of(k // NZ, k % NZ)), device_id_type=MESH)
    pl.semaphore_signal(barrier, inc=1, device_id=sibling, device_id_type=MESH)

    tiles[128] = jnp.zeros((TILE, TILE), BF)
    feats[pl.ds(a * 4, 4)] = x_ref[...].reshape(4, TILE, TILE)

    pl.semaphore_wait(barrier, 15)

    def gather(buf, s_sem, r_sem, s_fwd, r_fwd, use):
        def block(owner):
            return buf.at[pl.ds(owner * 4, 4)]

        def to_peer(k):
            peer = aa_of(k // 2, lax.rem(k, 2))
            return pltpu.make_async_remote_copy(
                src_ref=block(a), dst_ref=block(a), send_sem=s_sem.at[k], recv_sem=r_sem.at[k],
                device_id=(peer, b), device_id_type=MESH,
            )

        def forward(k):
            owner = aa_of(4 - k // 2, lax.rem(k, 2))
            return pltpu.make_async_remote_copy(
                src_ref=block(owner), dst_ref=block(owner), send_sem=s_fwd.at[k], recv_sem=r_fwd.at[k],
                device_id=sibling, device_id_type=MESH,
            )

        def start(i, carry):
            to_peer(8 - i).start()
            return carry

        lax.fori_loop(1, 8, start, 0)
        forward(0).start()
        if use is not None:
            use(a)
            forward(0).wait_recv()
            use(a + 1 - 2 * c)

        def pass_on(k, carry):
            to_peer(k).wait_recv()
            forward(k).start()
            if use is not None:
                use(aa_of(4 - k // 2, lax.rem(k, 2)))
            return carry

        lax.fori_loop(1, 8, pass_on, 0)

        def take(k, carry):
            forward(k).wait_recv()
            if use is not None:
                use(aa_of(4 - k // 2, lax.rem(k, 2)) + 1 - 2 * c)
            return carry

        lax.fori_loop(0 if use is None else 1, 8, take, 0)

        def finish():
            def body(k, carry):
                to_peer(k).wait_send()
                forward(k).wait_send()
                return carry

            lax.fori_loop(1, 8, body, 0)
            forward(0).wait_send()

        return finish

    finish_a = gather(feats, as_sem, ar_sem, fs_sem, fr_sem, None)
    tile_copy.wait()

    group = 4

    def pair_products(source, width, acc, store):
        acc[:, pl.ds(0, width)] = jnp.zeros((TILE, width), F32)

        def body(i, carry):
            running = acc[:, pl.ds(0, width)]
            for j in range(group):
                q = i * group + j
                left = jnp.concatenate([tiles[slot_at[2 * q]], tiles[slot_at[2 * q + 1]]], axis=1)
                right = jnp.concatenate([source[col_at[2 * q]], source[col_at[2 * q + 1]]], axis=0)
                running = running * keep[q] + jnp.dot(left, right, preferred_element_type=F32)
                store(q, running)
            acc[:, pl.ds(0, width)] = running
            return carry

        lax.fori_loop(0, PAIRS // group, body, 0)

    def each(count, body):
        def one(i, carry):
            body(i)
            return carry

        lax.fori_loop(0, count, one, 0)

    def layer_one(sums1, acc):
        sums1[PAIRS] = jnp.zeros((TILE, TILE), F32)

        def store1(q, value):
            sums1[q] = value

        pair_products(feats, TILE, acc, store1)

        def pick1(r):
            send_c[r] = sums1[last[r]].astype(send_c.dtype)

        each(RB, pick1)

    pl.run_scoped(layer_one, pltpu.VMEM((PAIRS + 1, TILE, TILE), F32), pltpu.VMEM((TILE, TILE), F32))

    def exchange_c(k):
        peer = ba_of(k // NZ, k % NZ)
        return pltpu.make_async_remote_copy(
            src_ref=send_c.at[pl.ds(peer * 4, 4)], dst_ref=recv_c.at[k - 1], send_sem=cs_sem.at[k], recv_sem=cr_sem.at[k],
            device_id=(a, peer), device_id_type=MESH,
        )

    for k in (6, 2, 5, 7, 1, 3, 4):
        exchange_c(k).start()
    total = send_c[pl.ds(b * 4, 4)].astype(F32)
    for k in (4, 1, 3, 5, 7, 2, 6):
        exchange_c(k).wait_recv()
        total = total + recv_c[k - 1].astype(F32)
    lows[pl.ds(a * 4, 4)] = total.astype(BF)
    for k in range(1, 8):
        exchange_c(k).wait_send()
    finish_a()

    zp, zm = (a, ba_of(0, 1)), (a, ba_of(0, 3))
    xn = (a, ba_of(1, 0))

    def message(i, offset, count, peer):
        return pltpu.make_async_remote_copy(
            src_ref=sb.at[pl.ds(offset, count)], dst_ref=rb.at[pl.ds(offset, count)],
            send_sem=es_sem.at[i], recv_sem=er_sem.at[i], device_id=peer, device_id_type=MESH,
        )

    m0p, m0m = message(0, M0P, N1, zp), message(1, M0M, N1, zm)
    xs2 = message(2, XS + 2 * N2, N2, xn)
    m1pb, m1ma = message(3, M1P + H1, H1, zp), message(4, M1M, H1, zm)
    xs1, xs3 = message(5, XS + N2, N2, xn), message(6, XS + 3 * N2, N2, xn)
    t2p, t2m = message(7, T2, H2, zp), message(8, T2 + H2, H2, zm)
    m1pa, m1mb = message(9, M1P, H1, zp), message(10, M1M + H1, H1, zm)
    m2p, m2m = message(11, M2P, N1, zp), message(12, M2M, N1, zm)
    t1b, t3a = message(13, T1 + H2, H2, zp), message(14, T3, H2, zm)
    t1a, t3b = message(15, T1, H2, zp), message(16, T3 + H2, H2, zm)
    xs0 = message(17, XS, N2, xn)
    xfa, xfb = message(18, XF, H1, xn), message(19, XF + H1, H1, xn)
    messages = [m0p, m0m, xs2, m1pb, m1ma, xs1, xs3, t2p, t2m, m1pa, m1mb, m2p, m2m, t1b, t3a, t1a, t3b, xs0, xfa, xfb]

    def layer_two(hid, proj_a, proj_b, sums2, acc):
        sums2[PAIRS] = jnp.zeros((TILE, 2 * TILE), BF)

        def columns(pair):
            (dx0, dz0), (dx1, dz1) = pair
            return jnp.concatenate([w2c[ba_of(dx0, dz0)], w2c[ba_of(dx1, dz1)]], axis=1)

        steps = (((0, 2), (1, 2)), ((1, 1), (1, 3)), ((0, 1), (0, 3)), ((0, 0), (1, 0)))

        def project(owner, s, proj):
            value = jnp.dot(hid[owner], columns(steps[s]), preferred_element_type=F32)
            proj[pl.ds(owner * 4, 4)] = value.astype(BF).reshape(4, TILE, 2 * TILE)

        def hidden_of(owner):
            rows = lows[pl.ds(owner * 4, 4)].reshape(4 * TILE, TILE)
            value = jnp.dot(rows, w1_ref[...], preferred_element_type=F32) + b1_ref[...]
            hid[owner] = jnp.maximum(value, 0.0).astype(BF)
            project(owner, 0, proj_a)
            project(owner, 1, proj_b)

        finish_d = gather(lows, ds_sem, dr_sem, gs_sem, gr_sem, hidden_of)
        finish_d()

        def store2(q, value):
            sums2[q] = value.astype(BF)

        def pick(r):
            value = sums2[last[r]].astype(F32)
            return value[:, :TILE], value[:, TILE:]

        def got(i):
            return rb[i].astype(F32)

        def put(i, value):
            sb[i] = value.astype(BF)

        pair_products(proj_a, 2 * TILE, acc, store2)

        def body(i):
            near, far = pick(i)
            put(M0P + i, near)
            put(M0P + H1 + i, far)
            near, far = pick(H1 + i)
            put(M0M + i, near)
            put(M0M + H1 + i, far)

        each(H1, body)
        m0p.start()
        m0m.start()

        def body(i):
            near, far = pick(N1 + i)
            put(T2 + i, near)
            put(XS + 2 * N2 + i, far)

        each(N2, body)
        xs2.start()

        pair_products(proj_b, 2 * TILE, acc, store2)

        def body(i):
            plus, minus = pick(N1 + i)
            put(XS + N2 + i, plus)
            put(XS + 3 * N2 + i, minus)

        each(N2, body)
        xs1.start()
        xs3.start()

        def body(i):
            put(M1M + i, pick(i)[1])
            put(M1P + H1 + i, pick(H1 + i)[0])

        each(H1, body)
        m1pb.start()
        m1ma.start()

        each(NA, lambda owner: project(owner, 2, proj_a))
        m0p.wait_recv()
        m0m.wait_recv()

        def body(i):
            put(M1P + i, pick(i)[0] + got(M0P + H1 + i))
            put(M1M + H1 + i, pick(H1 + i)[1] + got(M0M + H1 + i))

        each(H1, body)
        m1pa.start()
        m1mb.start()
        xs2.wait_recv()

        def body(i):
            put(T2 + i, sb[T2 + i].astype(F32) + got(XS + 2 * N2 + i))

        each(N2, body)
        t2p.start()
        t2m.start()

        pair_products(proj_a, 2 * TILE, acc, store2)

        def body(i):
            plus, minus = pick(i)
            put(M2P + i, plus + got(M0P + i))
            put(M2M + i, minus)
            plus, minus = pick(H1 + i)
            put(M2P + H1 + i, plus)
            put(M2M + H1 + i, minus + got(M0M + i))

        each(H1, body)
        m2p.start()
        m2m.start()
        xs1.wait_recv()
        xs3.wait_recv()

        def body(i):
            plus, minus = pick(N1 + i)
            put(T1 + i, plus + got(XS + N2 + i))
            put(T3 + i, minus + got(XS + 3 * N2 + i))

        each(N2, body)
        t1b.start()
        t3a.start()

        each(NA, lambda owner: project(owner, 3, proj_b))
        t2p.wait_recv()
        t2m.wait_recv()

        def body(i):
            put(T1 + i, sb[T1 + i].astype(F32) + got(T2 + i))
            put(T3 + H2 + i, sb[T3 + H2 + i].astype(F32) + got(T2 + H2 + i))

        each(H2, body)
        t1a.start()
        t3b.start()

        pair_products(proj_b, 2 * TILE, acc, store2)

        def body(i):
            put(XS + i, pick(N1 + i)[1])

        each(N2, body)
        xs0.start()
        m1pb.wait_recv()
        m1ma.wait_recv()
        m1pa.wait_recv()
        m1mb.wait_recv()

        def body(i):
            put(XF + i, pick(i)[1] + got(M1P + i) + got(M1M + i))

        each(H1, body)
        xfa.start()

        def body(i):
            j = H1 + i
            put(XF + j, pick(j)[1] + got(M1P + j) + got(M1M + j))

        each(H1, body)
        xfb.start()

        def write(r, value):
            out_ref[pl.ds(pl.multiple_of(r * TILE, TILE), TILE), :] = value.astype(BF)

        xs0.wait_recv()
        t1b.wait_recv()
        t1a.wait_recv()
        t3a.wait_recv()
        t3b.wait_recv()

        def body(i):
            write(N1 + i, pick(N1 + i)[0] + got(XS + i) + got(T1 + i) + got(T3 + i))

        each(N2, body)
        m2p.wait_recv()
        m2m.wait_recv()
        for start, copy in ((0, xfa), (H1, xfb)):
            copy.wait_recv()

            def body(i):
                j = start + i
                write(j, pick(j)[0] + got(M2P + j) + got(M2M + j) + got(XF + j))

            each(H1, body)
        for copy in messages:
            copy.wait_send()

    for copy in w2_copies:
        copy.wait()
    pl.run_scoped(
        layer_two,
        pltpu.VMEM((NA, 4 * TILE, 1024), BF),
        pltpu.VMEM((64, TILE, 2 * TILE), BF),
        pltpu.VMEM((64, TILE, 2 * TILE), BF),
        pltpu.VMEM((PAIRS + 1, TILE, 2 * TILE), BF),
        pltpu.VMEM((TILE, 2 * TILE), F32),
    )


def on_device(features, tile_values, tile_row, tile_col, weight_one, bias_one, weight_two):
    slot_at, col_at, keep, last = prepare(tile_row, tile_col)
    smem = pl.BlockSpec(memory_space=pltpu.SMEM)
    vmem = pl.BlockSpec(memory_space=pltpu.VMEM)
    hbm = pl.BlockSpec(memory_space=pl.ANY)
    dma = pltpu.SemaphoreType.DMA
    return pl.pallas_call(
        kernel,
        out_shape=jax.ShapeDtypeStruct((RB * TILE, TILE), BF),
        in_specs=[smem, smem, smem, smem, vmem, hbm, vmem, vmem, hbm],
        out_specs=vmem,
        scratch_shapes=[
            pltpu.VMEM((129, TILE, TILE), BF),
            pltpu.VMEM((NB, 1024, TILE), BF),
            pltpu.VMEM((64, TILE, TILE), BF),
            pltpu.VMEM((RB, TILE, TILE), CT),
            pltpu.VMEM((7, 4, TILE, TILE), CT),
            pltpu.VMEM((64, TILE, TILE), BF),
            pltpu.VMEM((BLOCKS, TILE, TILE), BF),
            pltpu.VMEM((BLOCKS, TILE, TILE), BF),
        ]
        + [dma((9,))]
        + [dma((8,))] * 10
        + [dma((20,))] * 2,
        compiler_params=pltpu.CompilerParams(
            collective_id=0, has_side_effects=True, vmem_limit_bytes=64 * 2**20 - 2**16
        ),
        cost_estimate=pl.CostEstimate(flops=26 * 10**9, bytes_accessed=8 * 2**20, transcendentals=0),
        name="two_layers",
    )(slot_at, col_at, keep, last, features, tile_values, weight_one, bias_one.reshape(1, -1), weight_two)


def solution(mesh):
    return jax.shard_map(
        on_device,
        mesh=mesh,
        in_specs=(
            P(("aa", "ba"), None),
            P(("aa", "ba"), None, None),
            P(("aa", "ba")),
            P(("aa", "ba")),
            P(),
            P(),
            P(),
        ),
        out_specs=P("aa", "ba"),
        check_vma=False,
    )
```

```python
import functools

import jax
import jax.numpy as jnp
from jax import lax
from jax.experimental import pallas as pl
from jax.experimental.pallas import tpu as pltpu
from jax.sharding import PartitionSpec as P

MESH = pl.DeviceIdType.MESH
TILE = 128
NZ = 4
NB = 8
NA = 16
RB = 32
N1 = 18
H1 = N1 // 2
N2 = RB - N1
H2 = N2 // 2
M0P, M0M, M1P, M1M, M2P, M2M = 0, N1, 2 * N1, 3 * N1, 4 * N1, 5 * N1
XS = 6 * N1
T2 = XS + 4 * N2
T1 = T2 + N2
T3 = T1 + N2
XF = T3 + N2
BLOCKS = XF + N1
PAIRS = 80
BF = jnp.bfloat16
F32 = jnp.float32
C_M0P, C_M0M, C_M1P, C_M1M, C_XS, C_T2, C_T1, C_T3, C_XF, C_BLOCKS = 0, 2, 4, 8, 12, 20, 22, 24, 26, 28


def prepare(tile_row, tile_col, index_v, keep_v):
    slots = TILE
    square = (slots, slots)

    def iota(dim, shape=square):
        return lax.broadcasted_iota(jnp.int32, shape, dim)

    def over_rows(x):
        return jnp.sum(x, axis=0, keepdims=True)

    def over_lanes(x):
        return jnp.sum(x, axis=1, keepdims=True)

    row_l = jnp.broadcast_to(jnp.where(tile_row < 0, -1, tile_row & (RB - 1)), square)
    clamped = jnp.maximum(tile_col, 0)
    col_l = jnp.broadcast_to((clamped >> 5) * 4 + (clamped & 3), square)
    row_s, col_s = row_l.T, col_l.T
    down, across = iota(0), iota(1)
    zero, one = jnp.zeros(square, jnp.int32), jnp.ones(square, jnp.int32)

    hot = row_s == across
    count_l = over_rows(jnp.where(hot, one, zero))
    count_s = over_lanes(jnp.where(row_l == down, one, zero))
    pairs_l, pairs_s = (count_l + 1) >> 1, (count_s + 1) >> 1
    start_l = over_rows(jnp.where(down < across, pairs_s, zero))
    start_s = over_lanes(jnp.where(across < down, pairs_l, zero))
    rank_s = over_lanes(jnp.where((row_l == row_s) & (across < down), one, zero))
    slot_start = over_lanes(jnp.where(hot, start_l, zero))
    place = jnp.where(row_s[:, :1] >= 0, 2 * slot_start + rank_s, -1)
    wide = (slots, 2 * TILE)
    match = place == iota(1, wide)
    nothing = jnp.zeros(wide, jnp.int32)
    slot_at = slots + over_rows(jnp.where(match, iota(0, wide) - slots, nothing))
    col_at = over_rows(jnp.where(match, col_s[:, :1], nothing))
    inside = (across > start_s) & (across < start_s + pairs_s)
    last = jnp.where(count_l > 0, start_l + pairs_l - 1, PAIRS)
    index_v[...] = jnp.zeros(index_v.shape, jnp.int32)
    index_v[0:1, :] = slot_at
    index_v[1:2, :] = col_at
    index_v[2:3, 0:TILE] = last
    keep_v[0:1, :] = over_rows(jnp.where(inside, one, zero)).astype(F32)


def kernel(
    row_ref, col_ref, x_ref, tiles_hbm, w1_ref, b1_ref, w2_hbm, out_ref,
    tiles, w2c, feats, cr, lows, sb, rb, index_v, keep_v, index, keeps,
    loc_sem, as_sem, ar_sem, fs_sem, fr_sem, cs_sem, cr_sem, ds_sem, dr_sem, gs_sem, gr_sem, es_sem, er_sem,
):
    a, b = lax.axis_index("aa"), lax.axis_index("ba")
    y, xh, c = a // 4, lax.rem(a // 2, 2), lax.rem(a, 2)
    xl, z = b // NZ, lax.rem(b, NZ)

    def aa_of(dy, dx):
        return lax.rem(y + dy, 4) * 4 + lax.rem(xh + dx, 2) * 2 + c

    def ba_of(dx, dz):
        return lax.rem(xl + dx, 2) * NZ + lax.rem(z + dz, NZ)

    sibling = (a + 1 - 2 * c, b)
    zp, zm = (a, ba_of(0, 1)), (a, ba_of(0, 3))
    xn = (a, ba_of(1, 0))

    tile_copy = pltpu.make_async_copy(tiles_hbm, tiles.at[pl.ds(0, 128)], loc_sem.at[0])
    tile_copy.start()
    w2_copies = []
    for f in range(NB):
        w2_copies.append(
            pltpu.make_async_copy(
                w2_hbm.at[:, pl.ds(f * TILE, TILE)],
                w2c.at[f],
                loc_sem.at[1 + f],
            )
        )
        w2_copies[-1].start()

    barrier = pltpu.get_barrier_semaphore()
    for k in range(1, 8):
        pl.semaphore_signal(barrier, inc=1, device_id=(aa_of(k // 2, k % 2), b), device_id_type=MESH)
    for peer in (sibling, zp, zm, xn):
        pl.semaphore_signal(barrier, inc=1, device_id=peer, device_id_type=MESH)

    tiles[128] = jnp.zeros((TILE, TILE), BF)
    feats[pl.ds(a * 4, 4)] = x_ref[...].reshape(4, TILE, TILE)

    prepare(row_ref[...], col_ref[...], index_v, keep_v)
    index_copy = pltpu.make_async_copy(index_v, index, loc_sem.at[9])
    keep_copy = pltpu.make_async_copy(keep_v, keeps, loc_sem.at[10])
    index_copy.start()
    keep_copy.start()
    pl.semaphore_wait(barrier, 11)

    def gather(buf, s_sem, r_sem, s_fwd, r_fwd, use):
        def block(owner):
            return buf.at[pl.ds(owner * 4, 4)]

        def to_peer(k):
            peer = aa_of(k // 2, lax.rem(k, 2))
            return pltpu.make_async_remote_copy(
                src_ref=block(a), dst_ref=block(a), send_sem=s_sem.at[k], recv_sem=r_sem.at[k],
                device_id=(peer, b), device_id_type=MESH,
            )

        def forward(k):
            owner = aa_of(4 - k // 2, lax.rem(k, 2))
            return pltpu.make_async_remote_copy(
                src_ref=block(owner), dst_ref=block(owner), send_sem=s_fwd.at[k], recv_sem=r_fwd.at[k],
                device_id=sibling, device_id_type=MESH,
            )

        for k in (1, 6, 2, 7, 3, 4, 5):
            to_peer(k).start()
        forward(0).start()

        def arrive(k):
            to_peer(k).wait_recv()
            forward(k).start()

        def owners(dy, same):
            here = aa_of(dy, 0), aa_of(dy, 1)
            return here if same else tuple(o + 1 - 2 * c for o in here)

        def siblings(dy):
            forward((8 - 2 * dy) % 8).wait_recv()
            forward((8 - 2 * dy) % 8 + 1).wait_recv()
            if use is not None:
                use(*owners(dy, False))

        before = None
        for dy in (0, 1, 3, 2):
            if dy > 0:
                arrive(8 - 2 * dy)
            arrive((8 - 2 * dy) % 8 + 1)
            if use is not None:
                use(*owners(dy, True))
            if before is not None:
                siblings(before)
            before = dy
        siblings(before)

        def finish():
            def body(k, carry):
                to_peer(k).wait_send()
                forward(k).wait_send()
                return carry

            lax.fori_loop(1, 8, body, 0)
            forward(0).wait_send()

        return finish

    finish_a = gather(feats, as_sem, ar_sem, fs_sem, fr_sem, None)
    tile_copy.wait()
    index_copy.wait()
    keep_copy.wait()

    group = 16

    def pair_products(source, offset, width, acc, store):
        acc[:, pl.ds(0, width)] = jnp.zeros((TILE, width), F32)

        def body(i, carry):
            running = acc[:, pl.ds(0, width)]
            for j in range(group):
                q = i * group + j
                left = jnp.concatenate([tiles[index[0, 2 * q]], tiles[index[0, 2 * q + 1]]], axis=1)
                cols = pl.ds(offset, width)
                right = jnp.concatenate([source[index[1, 2 * q], :, cols], source[index[1, 2 * q + 1], :, cols]], axis=0)
                running = running * keeps[0, q] + jnp.dot(left, right, preferred_element_type=F32)
                store(q, running)
            acc[:, pl.ds(0, width)] = running
            return carry

        lax.fori_loop(0, PAIRS // group, body, 0)

    def each(count, body):
        def one(i, carry):
            body(i)
            return carry

        lax.fori_loop(0, count, one, 0)

    def layer_one(sums1, acc, cs):
        sums1[PAIRS] = jnp.zeros((TILE, TILE), F32)

        def store1(q, value):
            sums1[q] = value

        pair_products(feats, 0, TILE, acc, store1)

        def own(dx, dz, j):
            return sums1[index[2, ba_of(dx, dz) * 4 + j]]

        def message(i, offset, count, peer):
            return pltpu.make_async_remote_copy(
                src_ref=cs.at[pl.ds(offset, count)], dst_ref=cr.at[pl.ds(offset, count)],
                send_sem=cs_sem.at[i], recv_sem=cr_sem.at[i], device_id=peer, device_id_type=MESH,
            )

        m0p, m0m = message(0, C_M0P, 2, zp), message(1, C_M0M, 2, zm)
        xsa, xsb = message(2, C_XS, 2, xn), message(3, C_XS + 2, 6, xn)
        m1pb, m1ma = message(4, C_M1P + 2, 2, zp), message(5, C_M1M, 2, zm)
        m1pa, m1mb = message(6, C_M1P, 2, zp), message(7, C_M1M + 2, 2, zm)
        t2p, t2m = message(8, C_T2, 1, zp), message(9, C_T2 + 1, 1, zm)
        t1b, t3a = message(10, C_T1 + 1, 1, zp), message(11, C_T3, 1, zm)
        t1a, t3b = message(12, C_T1, 1, zp), message(13, C_T3 + 1, 1, zm)
        xf = message(14, C_XF, 2, xn)

        for dx in range(2):
            cs[C_M0P + dx] = own(dx, 2, 0)
            cs[C_M0M + dx] = own(dx, 2, 1)
        m0p.start()
        m0m.start()
        for j in range(2):
            cs[C_XS + j] = own(1, 2, 2 + j)
        xsa.start()
        for j in range(2):
            cs[C_XS + 2 + j] = own(1, 1, 2 + j)
            cs[C_XS + 4 + j] = own(1, 3, 2 + j)
            cs[C_XS + 6 + j] = own(1, 0, 2 + j)
        xsb.start()
        for dx in range(2):
            cs[C_M1P + 2 + dx] = own(dx, 1, 1)
            cs[C_M1M + dx] = own(dx, 3, 0)
        m1pb.start()
        m1ma.start()
        xsa.wait_recv()
        for j in range(2):
            cs[C_T2 + j] = own(0, 2, 2 + j) + cr[C_XS + j]
        t2p.start()
        t2m.start()
        m0p.wait_recv()
        m0m.wait_recv()
        for dx in range(2):
            cs[C_M1P + dx] = own(dx, 1, 0) + cr[C_M0P + dx]
            cs[C_M1M + 2 + dx] = own(dx, 3, 1) + cr[C_M0M + dx]
        m1pa.start()
        m1mb.start()
        xsb.wait_recv()
        cs[C_T1 + 1] = own(0, 1, 3) + cr[C_XS + 3]
        cs[C_T3] = own(0, 3, 2) + cr[C_XS + 4]
        t1b.start()
        t3a.start()
        t2p.wait_recv()
        t2m.wait_recv()
        cs[C_T1] = own(0, 1, 2) + cr[C_XS + 2] + cr[C_T2]
        cs[C_T3 + 1] = own(0, 3, 3) + cr[C_XS + 5] + cr[C_T2 + 1]
        t1a.start()
        t3b.start()
        for copy in (m1pb, m1ma, m1pa, m1mb):
            copy.wait_recv()
        for j in range(2):
            cs[C_XF + j] = own(1, 0, j) + cr[C_M1P + 2 * j + 1] + cr[C_M1M + 2 * j + 1]
        xf.start()
        for copy in (t1b, t3a, t1a, t3b):
            copy.wait_recv()
        for j in range(2):
            value = own(0, 0, 2 + j) + cr[C_XS + 6 + j] + cr[C_T1 + j] + cr[C_T3 + j]
            lows[a * 4 + 2 + j] = value.astype(BF)
        xf.wait_recv()
        for j in range(2):
            value = own(0, 0, j) + cr[C_M1P + 2 * j] + cr[C_M1M + 2 * j] + cr[C_XF + j]
            lows[a * 4 + j] = value.astype(BF)
        for copy in (m0p, m0m, xsa, xsb, m1pb, m1ma, m1pa, m1mb, t2p, t2m, t1b, t3a, t1a, t3b, xf):
            copy.wait_send()

    pl.run_scoped(
        layer_one,
        pltpu.VMEM((PAIRS + 1, TILE, TILE), F32),
        pltpu.VMEM((TILE, TILE), F32),
        pltpu.VMEM((C_BLOCKS, TILE, TILE), F32),
    )
    finish_a()


    def message(i, offset, count, peer):
        return pltpu.make_async_remote_copy(
            src_ref=sb.at[pl.ds(offset, count)], dst_ref=rb.at[pl.ds(offset, count)],
            send_sem=es_sem.at[i], recv_sem=er_sem.at[i], device_id=peer, device_id_type=MESH,
        )

    m0p, m0m = message(0, M0P, N1, zp), message(1, M0M, N1, zm)
    xs2 = message(2, XS + 2 * N2, N2, xn)
    m1pb, m1ma = message(3, M1P + H1, H1, zp), message(4, M1M, H1, zm)
    xs1, xs3 = message(5, XS + N2, N2, xn), message(6, XS + 3 * N2, N2, xn)
    t2p, t2m = message(7, T2, H2, zp), message(8, T2 + H2, H2, zm)
    m1pa, m1mb = message(9, M1P, H1, zp), message(10, M1M + H1, H1, zm)
    m2p, m2m = message(11, M2P, N1, zp), message(12, M2M, N1, zm)
    t1b, t3a = message(13, T1 + H2, H2, zp), message(14, T3, H2, zm)
    t1a, t3b = message(15, T1, H2, zp), message(16, T3 + H2, H2, zm)
    xs0 = message(17, XS, N2, xn)
    xfa, xfb = message(18, XF, H1, xn), message(19, XF + H1, H1, xn)
    messages = [m0p, m0m, xs2, m1pb, m1ma, xs1, xs3, t2p, t2m, m1pa, m1mb, m2p, m2m, t1b, t3a, t1a, t3b, xs0, xfa, xfb]

    def layer_two(hid, proj, sums2, acc):
        sums2[PAIRS] = jnp.zeros((TILE, 2 * TILE), BF)

        def columns(half):
            places = (((0, 2), (1, 2), (1, 1), (1, 3)), ((0, 1), (0, 3), (0, 0), (1, 0)))[half]
            return jnp.concatenate([w2c[ba_of(dx, dz)] for dx, dz in places], axis=1)

        def project(rows, half):
            return jnp.dot(rows, columns(half), preferred_element_type=F32).astype(BF)

        def hidden_of(one, two):
            rows = [lows[pl.ds(o * 4, 4)].reshape(4 * TILE, TILE) for o in (one, two)]
            value = jnp.dot(jnp.concatenate(rows, axis=0), w1_ref[...], preferred_element_type=F32) + b1_ref[...]
            value = jnp.maximum(value, 0.0).astype(BF)
            hid[one] = value[: 4 * TILE]
            hid[two] = value[4 * TILE :]
            value = project(value, 0).reshape(8, TILE, 4 * TILE)
            proj[pl.ds(one * 4, 4)] = value[:4]
            proj[pl.ds(two * 4, 4)] = value[4:]

        finish_d = gather(lows, ds_sem, dr_sem, gs_sem, gr_sem, hidden_of)
        finish_d()

        def store2(q, value):
            sums2[q] = value.astype(BF)

        def pick(r):
            value = sums2[index[2, r]].astype(F32)
            return value[:, :TILE], value[:, TILE:]

        def got(i):
            return rb[i].astype(F32)

        def put(i, value):
            sb[i] = value.astype(BF)

        pair_products(proj, 0 * TILE, 2 * TILE, acc, store2)

        def body(i):
            near, far = pick(i)
            put(M0P + i, near)
            put(M0P + H1 + i, far)
            near, far = pick(H1 + i)
            put(M0M + i, near)
            put(M0M + H1 + i, far)

        each(H1, body)
        m0p.start()
        m0m.start()

        def body(i):
            near, far = pick(N1 + i)
            put(T2 + i, near)
            put(XS + 2 * N2 + i, far)

        each(N2, body)
        xs2.start()

        pair_products(proj, 2 * TILE, 2 * TILE, acc, store2)

        def body(i):
            plus, minus = pick(N1 + i)
            put(XS + N2 + i, plus)
            put(XS + 3 * N2 + i, minus)

        each(N2, body)
        xs1.start()
        xs3.start()

        def body(i):
            put(M1M + i, pick(i)[1])
            put(M1P + H1 + i, pick(H1 + i)[0])

        each(H1, body)
        m1pb.start()
        m1ma.start()

        def body(i):
            rows = hid[pl.ds(2 * i, 2)].reshape(8 * TILE, 1024)
            proj[pl.ds(8 * i, 8)] = project(rows, 1).reshape(8, TILE, 4 * TILE)

        each(NA // 2, body)
        m0p.wait_recv()
        m0m.wait_recv()

        def body(i):
            put(M1P + i, pick(i)[0] + got(M0P + H1 + i))
            put(M1M + H1 + i, pick(H1 + i)[1] + got(M0M + H1 + i))

        each(H1, body)
        m1pa.start()
        m1mb.start()
        xs2.wait_recv()

        def body(i):
            put(T2 + i, sb[T2 + i].astype(F32) + got(XS + 2 * N2 + i))

        each(N2, body)
        t2p.start()
        t2m.start()

        pair_products(proj, 0 * TILE, 2 * TILE, acc, store2)

        def body(i):
            plus, minus = pick(i)
            put(M2P + i, plus + got(M0P + i))
            put(M2M + i, minus)
            plus, minus = pick(H1 + i)
            put(M2P + H1 + i, plus)
            put(M2M + H1 + i, minus + got(M0M + i))

        each(H1, body)
        m2p.start()
        m2m.start()
        xs1.wait_recv()
        xs3.wait_recv()

        def body(i):
            plus, minus = pick(N1 + i)
            put(T1 + i, plus + got(XS + N2 + i))
            put(T3 + i, minus + got(XS + 3 * N2 + i))

        each(N2, body)
        t1b.start()
        t3a.start()

        t2p.wait_recv()
        t2m.wait_recv()

        def body(i):
            put(T1 + i, sb[T1 + i].astype(F32) + got(T2 + i))
            put(T3 + H2 + i, sb[T3 + H2 + i].astype(F32) + got(T2 + H2 + i))

        each(H2, body)
        t1a.start()
        t3b.start()

        pair_products(proj, 2 * TILE, 2 * TILE, acc, store2)

        def body(i):
            put(XS + i, pick(N1 + i)[1])

        each(N2, body)
        xs0.start()
        m1pb.wait_recv()
        m1ma.wait_recv()
        m1pa.wait_recv()
        m1mb.wait_recv()

        def body(i):
            put(XF + i, pick(i)[1] + got(M1P + i) + got(M1M + i))

        each(H1, body)
        xfa.start()

        def body(i):
            j = H1 + i
            put(XF + j, pick(j)[1] + got(M1P + j) + got(M1M + j))

        each(H1, body)
        xfb.start()

        def write(r, value):
            out_ref[pl.ds(pl.multiple_of(r * TILE, TILE), TILE), :] = value.astype(BF)

        xs0.wait_recv()
        t1b.wait_recv()
        t1a.wait_recv()
        t3a.wait_recv()
        t3b.wait_recv()

        def body(i):
            write(N1 + i, pick(N1 + i)[0] + got(XS + i) + got(T1 + i) + got(T3 + i))

        each(N2, body)
        m2p.wait_recv()
        m2m.wait_recv()
        for start, copy in ((0, xfa), (H1, xfb)):
            copy.wait_recv()

            def body(i):
                j = start + i
                write(j, pick(j)[0] + got(M2P + j) + got(M2M + j) + got(XF + j))

            each(H1, body)
        for copy in messages:
            copy.wait_send()

    for copy in w2_copies:
        copy.wait()
    pl.run_scoped(
        layer_two,
        pltpu.VMEM((NA, 4 * TILE, 1024), BF),
        pltpu.VMEM((64, TILE, 4 * TILE), BF),
        pltpu.VMEM((PAIRS + 1, TILE, 2 * TILE), BF),
        pltpu.VMEM((TILE, 2 * TILE), F32),
    )


def on_device(features, tile_values, tile_row, tile_col, weight_one, bias_one, weight_two):
    vmem = pl.BlockSpec(memory_space=pltpu.VMEM)
    hbm = pl.BlockSpec(memory_space=pl.ANY)
    dma = pltpu.SemaphoreType.DMA
    return pl.pallas_call(
        kernel,
        out_shape=jax.ShapeDtypeStruct((RB * TILE, TILE), BF),
        in_specs=[vmem, vmem, vmem, hbm, vmem, vmem, hbm],
        out_specs=vmem,
        scratch_shapes=[
            pltpu.VMEM((129, TILE, TILE), BF),
            pltpu.VMEM((NB, 1024, TILE), BF),
            pltpu.VMEM((64, TILE, TILE), BF),
            pltpu.VMEM((C_BLOCKS, TILE, TILE), F32),
            pltpu.VMEM((64, TILE, TILE), BF),
            pltpu.VMEM((BLOCKS, TILE, TILE), BF),
            pltpu.VMEM((BLOCKS, TILE, TILE), BF),
            pltpu.VMEM((8, 2 * TILE), jnp.int32),
            pltpu.VMEM((8, TILE), F32),
            pltpu.SMEM((8, 2 * TILE), jnp.int32),
            pltpu.SMEM((8, TILE), F32),
        ]
        + [dma((11,))]
        + [dma((8,))] * 4
        + [dma((15,))] * 2
        + [dma((8,))] * 4
        + [dma((20,))] * 2,
        compiler_params=pltpu.CompilerParams(
            collective_id=0, has_side_effects=True, vmem_limit_bytes=64 * 2**20 - 2**16
        ),
        cost_estimate=pl.CostEstimate(flops=26 * 10**9, bytes_accessed=8 * 2**20, transcendentals=0),
        name="two_layers",
    )(tile_row.reshape(1, -1), tile_col.reshape(1, -1), features, tile_values, weight_one, bias_one.reshape(1, -1), weight_two)


def solution(mesh):
    return jax.shard_map(
        on_device,
        mesh=mesh,
        in_specs=(
            P(("aa", "ba"), None),
            P(("aa", "ba"), None, None),
            P(("aa", "ba")),
            P(("aa", "ba")),
            P(),
            P(),
            P(),
        ),
        out_specs=P("aa", "ba"),
        check_vma=False,
    )
```

```python
import functools

import jax
import jax.numpy as jnp
from jax import lax
from jax.experimental import pallas as pl
from jax.experimental.pallas import tpu as pltpu
from jax.sharding import PartitionSpec as P

MESH = pl.DeviceIdType.MESH
TILE = 128
NZ = 4
NB = 8
NA = 16
RB = 32
N1 = 18
H1 = N1 // 2
N2 = RB - N1
H2 = N2 // 2
M0P, M0M, M1P, M1M, M2P, M2M = 0, N1, 2 * N1, 3 * N1, 4 * N1, 5 * N1
XS = 6 * N1
T2 = XS + 4 * N2
T1 = T2 + N2
T3 = T1 + N2
XF = T3 + N2
BLOCKS = XF + N1
PAIRS = 80
BF = jnp.bfloat16
F32 = jnp.float32
C_M0P, C_M0M, C_M1P, C_M1M, C_XS, C_T2, C_T1, C_T3, C_XF, C_BLOCKS = 0, 2, 4, 8, 12, 20, 22, 24, 26, 28


def prepare(tile_row, tile_col, index_v, keep_v):
    slots = TILE
    square = (slots, slots)

    def iota(dim, shape=square):
        return lax.broadcasted_iota(jnp.int32, shape, dim)

    def over_rows(x):
        return jnp.sum(x, axis=0, keepdims=True)

    def over_lanes(x):
        return jnp.sum(x, axis=1, keepdims=True)

    row_l = jnp.broadcast_to(jnp.where(tile_row < 0, -1, tile_row & (RB - 1)), square)
    clamped = jnp.maximum(tile_col, 0)
    col_l = jnp.broadcast_to((clamped >> 5) * 4 + (clamped & 3), square)
    row_s, col_s = row_l.T, col_l.T
    down, across = iota(0), iota(1)
    zero, one = jnp.zeros(square, jnp.int32), jnp.ones(square, jnp.int32)

    hot = row_s == across
    count_l = over_rows(jnp.where(hot, one, zero))
    count_s = over_lanes(jnp.where(row_l == down, one, zero))
    pairs_l, pairs_s = (count_l + 1) >> 1, (count_s + 1) >> 1
    start_l = over_rows(jnp.where(down < across, pairs_s, zero))
    start_s = over_lanes(jnp.where(across < down, pairs_l, zero))
    rank_s = over_lanes(jnp.where((row_l == row_s) & (across < down), one, zero))
    slot_start = over_lanes(jnp.where(hot, start_l, zero))
    place = jnp.where(row_s[:, :1] >= 0, 2 * slot_start + rank_s, -1)
    wide = (slots, 2 * TILE)
    match = place == iota(1, wide)
    nothing = jnp.zeros(wide, jnp.int32)
    slot_at = slots + over_rows(jnp.where(match, iota(0, wide) - slots, nothing))
    col_at = over_rows(jnp.where(match, col_s[:, :1], nothing))
    inside = (across > start_s) & (across < start_s + pairs_s)
    last = jnp.where(count_l > 0, start_l + pairs_l - 1, PAIRS)
    index_v[...] = jnp.zeros(index_v.shape, jnp.int32)
    index_v[0:1, :] = slot_at
    index_v[1:2, :] = col_at
    index_v[2:3, 0:TILE] = last
    keep_v[0:1, :] = over_rows(jnp.where(inside, one, zero)).astype(F32)


def kernel(
    row_hbm, col_hbm, x_hbm, tiles_hbm, w1_hbm, b1_hbm, w2_hbm, out_hbm,
    tiles, w2c, feats, cr, lows, sb, rb, index_v, keep_v, index, keeps, row_ref, col_ref, w1_ref, b1_ref, out_ref,
    loc_sem, as_sem, ar_sem, fs_sem, fr_sem, cs_sem, cr_sem, ds_sem, dr_sem, gs_sem, gr_sem, es_sem, er_sem,
):
    a, b = lax.axis_index("aa"), lax.axis_index("ba")
    y, xh, c = a // 4, lax.rem(a // 2, 2), lax.rem(a, 2)
    xl, z = b // NZ, lax.rem(b, NZ)

    def aa_of(dy, dx):
        return lax.rem(y + dy, 4) * 4 + lax.rem(xh + dx, 2) * 2 + c

    def ba_of(dx, dz):
        return lax.rem(xl + dx, 2) * NZ + lax.rem(z + dz, NZ)

    sibling = (a + 1 - 2 * c, b)
    zp, zm = (a, ba_of(0, 1)), (a, ba_of(0, 3))
    xn = (a, ba_of(1, 0))

    barrier = pltpu.get_barrier_semaphore()
    for k in (4, 1, 2, 6):
        pl.semaphore_signal(barrier, inc=1, device_id=(aa_of(k // 2, k % 2), b), device_id_type=MESH)
    for peer in (sibling, zp, zm, xn):
        pl.semaphore_signal(barrier, inc=1, device_id=peer, device_id_type=MESH)

    early = [
        pltpu.make_async_copy(x_hbm, feats.at[pl.ds(a * 4, 4)], loc_sem.at[11]),
        pltpu.make_async_copy(row_hbm, row_ref, loc_sem.at[12]),
        pltpu.make_async_copy(col_hbm, col_ref, loc_sem.at[13]),
    ]
    late = [
        pltpu.make_async_copy(w1_hbm, w1_ref, loc_sem.at[14]),
        pltpu.make_async_copy(b1_hbm, b1_ref, loc_sem.at[15]),
    ]
    for copy in early + late:
        copy.start()
    tile_copy = pltpu.make_async_copy(tiles_hbm, tiles.at[pl.ds(0, 128)], loc_sem.at[0])
    tile_copy.start()
    w2_copies = []
    for f in range(NB):
        w2_copies.append(
            pltpu.make_async_copy(
                w2_hbm.at[:, pl.ds(f * TILE, TILE)],
                w2c.at[f],
                loc_sem.at[1 + f],
            )
        )
        w2_copies[-1].start()

    tiles[128] = jnp.zeros((TILE, TILE), BF)

    early[0].wait()
    pl.semaphore_wait(barrier, 8)

    def gather(buf, s_sem, r_sem, s_fwd, r_fwd, use, between=None):
        def block(owner):
            return buf.at[pl.ds(owner * 4, 4)]

        def remote(i, ref, peer):
            return pltpu.make_async_remote_copy(
                src_ref=ref, dst_ref=ref, send_sem=s_sem.at[i], recv_sem=r_sem.at[i],
                device_id=(peer, b), device_id_type=MESH,
            )

        def to_peer(k):
            return remote(k, block(a), aa_of(k // 2, k % 2))

        def first_half(dy):
            return remote(2 * dy + 1, buf.at[pl.ds(aa_of(0, 1) * 4, 2)], aa_of(dy, 0))

        def second_half(dy):
            return remote(8 + dy, buf.at[pl.ds(aa_of(4 - dy, 0) * 4 + 2, 2)], aa_of(0, 1))

        def forward(k):
            owner = aa_of(4 - k // 2, lax.rem(k, 2))
            return pltpu.make_async_remote_copy(
                src_ref=block(owner), dst_ref=block(owner), send_sem=s_fwd.at[k], recv_sem=r_fwd.at[k],
                device_id=sibling, device_id_type=MESH,
            )

        for k in (1, 6, 2, 4):
            to_peer(k).start()
        forward(0).start()

        if between is not None:
            between()

        def own(k, l):
            if use is not None:
                use(aa_of(4 - k // 2, k % 2), aa_of(4 - l // 2, l % 2))

        def other(k, l):
            forward(k).wait_recv()
            forward(l).wait_recv()
            if use is not None:
                use(aa_of(4 - k // 2, k % 2) + 1 - 2 * c, aa_of(4 - l // 2, l % 2) + 1 - 2 * c)

        to_peer(1).wait_recv()
        for dy in (2, 1, 3):
            first_half(dy).start()
        forward(1).start()
        own(0, 1)
        for dy in (1, 3):
            to_peer(2 * dy).wait_recv()
            second_half(dy).start()
            forward(2 * dy).start()
        own(2, 6)
        to_peer(4).wait_recv()
        second_half(2).start()
        forward(4).start()
        other(0, 1)
        other(2, 6)
        for dy in (1, 3):
            first_half(dy).wait_recv()
            second_half(dy).wait_recv()
            forward(2 * dy + 1).start()
        own(4, 3)
        first_half(2).wait_recv()
        second_half(2).wait_recv()
        forward(5).start()
        own(7, 5)
        other(4, 3)
        other(7, 5)

        def finish():
            for k in (1, 2, 4, 6):
                to_peer(k).wait_send()
            for dy in (1, 2, 3):
                first_half(dy).wait_send()
                second_half(dy).wait_send()
            for k in range(8):
                forward(k).wait_send()

        return finish

    index_copy = pltpu.make_async_copy(index_v, index, loc_sem.at[9])
    keep_copy = pltpu.make_async_copy(keep_v, keeps, loc_sem.at[10])

    def order():
        early[1].wait()
        early[2].wait()
        prepare(row_ref[...], col_ref[...], index_v, keep_v)
        index_copy.start()
        keep_copy.start()

    finish_a = gather(feats, as_sem, ar_sem, fs_sem, fr_sem, None, order)
    tile_copy.wait()
    index_copy.wait()
    keep_copy.wait()

    group = 16

    def pair_products(source, offset, width, acc, store):
        acc[:, pl.ds(0, width)] = jnp.zeros((TILE, width), F32)

        def body(i, carry):
            running = acc[:, pl.ds(0, width)]
            for j in range(group):
                q = i * group + j
                left = jnp.concatenate([tiles[index[0, 2 * q]], tiles[index[0, 2 * q + 1]]], axis=1)
                cols = pl.ds(offset, width)
                right = jnp.concatenate([source[index[1, 2 * q], :, cols], source[index[1, 2 * q + 1], :, cols]], axis=0)
                running = running * keeps[0, q] + jnp.dot(left, right, preferred_element_type=F32)
                store(q, running)
            acc[:, pl.ds(0, width)] = running
            return carry

        lax.fori_loop(0, PAIRS // group, body, 0)

    def each(count, body):
        def one(i, carry):
            body(i)
            return carry

        lax.fori_loop(0, count, one, 0)

    def layer_one(sums1, acc, cs):
        sums1[PAIRS] = jnp.zeros((TILE, TILE), F32)

        def store1(q, value):
            sums1[q] = value

        pair_products(feats, 0, TILE, acc, store1)

        def own(dx, dz, j):
            return sums1[index[2, ba_of(dx, dz) * 4 + j]]

        def message(i, offset, count, peer):
            return pltpu.make_async_remote_copy(
                src_ref=cs.at[pl.ds(offset, count)], dst_ref=cr.at[pl.ds(offset, count)],
                send_sem=cs_sem.at[i], recv_sem=cr_sem.at[i], device_id=peer, device_id_type=MESH,
            )

        m0p, m0m = message(0, C_M0P, 2, zp), message(1, C_M0M, 2, zm)
        xsa, xsb = message(2, C_XS, 2, xn), message(3, C_XS + 2, 6, xn)
        m1pb, m1ma = message(4, C_M1P + 2, 2, zp), message(5, C_M1M, 2, zm)
        m1pa, m1mb = message(6, C_M1P, 2, zp), message(7, C_M1M + 2, 2, zm)
        t2p, t2m = message(8, C_T2, 1, zp), message(9, C_T2 + 1, 1, zm)
        t1b, t3a = message(10, C_T1 + 1, 1, zp), message(11, C_T3, 1, zm)
        t1a, t3b = message(12, C_T1, 1, zp), message(13, C_T3 + 1, 1, zm)
        xf = message(14, C_XF, 2, xn)

        for dx in range(2):
            cs[C_M0P + dx] = own(dx, 2, 0)
            cs[C_M0M + dx] = own(dx, 2, 1)
        m0p.start()
        m0m.start()
        for j in range(2):
            cs[C_XS + j] = own(1, 2, 2 + j)
        xsa.start()
        for j in range(2):
            cs[C_XS + 2 + j] = own(1, 1, 2 + j)
            cs[C_XS + 4 + j] = own(1, 3, 2 + j)
            cs[C_XS + 6 + j] = own(1, 0, 2 + j)
        xsb.start()
        for dx in range(2):
            cs[C_M1P + 2 + dx] = own(dx, 1, 1)
            cs[C_M1M + dx] = own(dx, 3, 0)
        m1pb.start()
        m1ma.start()
        xsa.wait_recv()
        for j in range(2):
            cs[C_T2 + j] = own(0, 2, 2 + j) + cr[C_XS + j]
        t2p.start()
        t2m.start()
        m0p.wait_recv()
        m0m.wait_recv()
        for dx in range(2):
            cs[C_M1P + dx] = own(dx, 1, 0) + cr[C_M0P + dx]
            cs[C_M1M + 2 + dx] = own(dx, 3, 1) + cr[C_M0M + dx]
        m1pa.start()
        m1mb.start()
        xsb.wait_recv()
        cs[C_T1 + 1] = own(0, 1, 3) + cr[C_XS + 3]
        cs[C_T3] = own(0, 3, 2) + cr[C_XS + 4]
        t1b.start()
        t3a.start()
        t2p.wait_recv()
        t2m.wait_recv()
        cs[C_T1] = own(0, 1, 2) + cr[C_XS + 2] + cr[C_T2]
        cs[C_T3 + 1] = own(0, 3, 3) + cr[C_XS + 5] + cr[C_T2 + 1]
        t1a.start()
        t3b.start()
        for copy in (m1pb, m1ma, m1pa, m1mb):
            copy.wait_recv()
        for j in range(2):
            cs[C_XF + j] = own(1, 0, j) + cr[C_M1P + 2 * j + 1] + cr[C_M1M + 2 * j + 1]
        xf.start()
        for copy in (t1b, t3a, t1a, t3b):
            copy.wait_recv()
        for j in range(2):
            value = own(0, 0, 2 + j) + cr[C_XS + 6 + j] + cr[C_T1 + j] + cr[C_T3 + j]
            lows[a * 4 + 2 + j] = value.astype(BF)
        xf.wait_recv()
        for j in range(2):
            value = own(0, 0, j) + cr[C_M1P + 2 * j] + cr[C_M1M + 2 * j] + cr[C_XF + j]
            lows[a * 4 + j] = value.astype(BF)
        for copy in (m0p, m0m, xsa, xsb, m1pb, m1ma, m1pa, m1mb, t2p, t2m, t1b, t3a, t1a, t3b, xf):
            copy.wait_send()

    pl.run_scoped(
        layer_one,
        pltpu.VMEM((PAIRS + 1, TILE, TILE), F32),
        pltpu.VMEM((TILE, TILE), F32),
        pltpu.VMEM((C_BLOCKS, TILE, TILE), F32),
    )
    finish_a()


    def message(i, offset, count, peer):
        return pltpu.make_async_remote_copy(
            src_ref=sb.at[pl.ds(offset, count)], dst_ref=rb.at[pl.ds(offset, count)],
            send_sem=es_sem.at[i], recv_sem=er_sem.at[i], device_id=peer, device_id_type=MESH,
        )

    m0p, m0m = message(0, M0P, N1, zp), message(1, M0M, N1, zm)
    xs2 = message(2, XS + 2 * N2, N2, xn)
    m1pb, m1ma = message(3, M1P + H1, H1, zp), message(4, M1M, H1, zm)
    xs1, xs3 = message(5, XS + N2, N2, xn), message(6, XS + 3 * N2, N2, xn)
    t2p, t2m = message(7, T2, H2, zp), message(8, T2 + H2, H2, zm)
    m1pa, m1mb = message(9, M1P, H1, zp), message(10, M1M + H1, H1, zm)
    m2p, m2m = message(11, M2P, N1, zp), message(12, M2M, N1, zm)
    t1, t3 = message(13, T1, N2, zp), message(14, T3, N2, zm)
    xs0 = message(15, XS, N2, xn)
    xfa, xfb = message(16, XF, H1, xn), message(17, XF + H1, H1, xn)
    messages = [m0p, m0m, xs2, m1pb, m1ma, xs1, xs3, t2p, t2m, m1pa, m1mb, m2p, m2m, t1, t3, xs0, xfa, xfb]

    def layer_two(hid, proj, sums2, acc):
        sums2[PAIRS] = jnp.zeros((TILE, 2 * TILE), BF)

        def columns(s):
            places = (((0, 2), (1, 2)), ((1, 1), (1, 3)), ((0, 1), (0, 3)), ((0, 0), (1, 0)))[s]
            return jnp.concatenate([w2c[ba_of(dx, dz)] for dx, dz in places], axis=1)

        def project(rows, s):
            return jnp.dot(rows, columns(s), preferred_element_type=F32).astype(BF)

        def project_all(s):
            def body(i):
                rows = hid[pl.ds(4 * i, 4)].reshape(16 * TILE, 1024)
                value = project(rows, s).reshape(16, TILE, 2 * TILE)
                proj[pl.ds(16 * i, 16), :, pl.ds(s % 2 * 2 * TILE, 2 * TILE)] = value

            each(NA // 4, body)

        def hidden_of(one, two):
            rows = [lows[pl.ds(o * 4, 4)].reshape(4 * TILE, TILE) for o in (one, two)]
            value = jnp.dot(jnp.concatenate(rows, axis=0), w1_ref[...], preferred_element_type=F32) + b1_ref[...]
            value = jnp.maximum(value, 0.0).astype(BF)
            hid[one] = value[: 4 * TILE]
            hid[two] = value[4 * TILE :]
            value = project(value, 0).reshape(8, TILE, 2 * TILE)
            proj[pl.ds(one * 4, 4), :, pl.ds(0, 2 * TILE)] = value[:4]
            proj[pl.ds(two * 4, 4), :, pl.ds(0, 2 * TILE)] = value[4:]

        finish_d = gather(lows, ds_sem, dr_sem, gs_sem, gr_sem, hidden_of)
        finish_d()

        def store2(q, value):
            sums2[q] = value.astype(BF)

        def pick(r):
            value = sums2[index[2, r]].astype(F32)
            return value[:, :TILE], value[:, TILE:]

        def got(i):
            return rb[i].astype(F32)

        def put(i, value):
            sb[i] = value.astype(BF)

        pair_products(proj, 0 * TILE, 2 * TILE, acc, store2)

        def body(i):
            near, far = pick(i)
            put(M0P + i, near)
            put(M0P + H1 + i, far)
            near, far = pick(H1 + i)
            put(M0M + i, near)
            put(M0M + H1 + i, far)

        each(H1, body)
        m0p.start()
        m0m.start()

        def body(i):
            near, far = pick(N1 + i)
            put(T2 + i, near)
            put(XS + 2 * N2 + i, far)

        each(N2, body)
        xs2.start()

        project_all(1)

        pair_products(proj, 2 * TILE, 2 * TILE, acc, store2)

        def body(i):
            plus, minus = pick(N1 + i)
            put(XS + N2 + i, plus)
            put(XS + 3 * N2 + i, minus)

        each(N2, body)
        xs1.start()
        xs3.start()

        def body(i):
            put(M1M + i, pick(i)[1])
            put(M1P + H1 + i, pick(H1 + i)[0])

        each(H1, body)
        m1pb.start()
        m1ma.start()

        project_all(2)
        m0p.wait_recv()
        m0m.wait_recv()

        def body(i):
            put(M1P + i, pick(i)[0] + got(M0P + H1 + i))
            put(M1M + H1 + i, pick(H1 + i)[1] + got(M0M + H1 + i))

        each(H1, body)
        m1pa.start()
        m1mb.start()
        xs2.wait_recv()

        def body(i):
            put(T2 + i, sb[T2 + i].astype(F32) + got(XS + 2 * N2 + i))

        each(N2, body)
        t2p.start()
        t2m.start()

        pair_products(proj, 0 * TILE, 2 * TILE, acc, store2)

        def body(i):
            plus, minus = pick(i)
            put(M2P + i, plus + got(M0P + i))
            put(M2M + i, minus)
            plus, minus = pick(H1 + i)
            put(M2P + H1 + i, plus)
            put(M2M + H1 + i, minus + got(M0M + i))

        each(H1, body)
        m2p.start()
        m2m.start()

        def body(i):
            plus, minus = pick(N1 + i)
            put(T1 + i, plus)
            put(T3 + i, minus)

        each(N2, body)
        project_all(3)

        pair_products(proj, 2 * TILE, 2 * TILE, acc, store2)

        def body(i):
            put(XS + i, pick(N1 + i)[1])

        each(N2, body)
        xs0.start()
        m1pb.wait_recv()
        m1ma.wait_recv()
        m1pa.wait_recv()
        m1mb.wait_recv()

        def body(i):
            put(XF + i, pick(i)[1] + got(M1P + i) + got(M1M + i))

        each(H1, body)
        xfa.start()

        def body(i):
            j = H1 + i
            put(XF + j, pick(j)[1] + got(M1P + j) + got(M1M + j))

        each(H1, body)
        xfb.start()

        for copy in (xs1, xs3, t2p, t2m):
            copy.wait_recv()

        def body(i):
            j = H2 + i
            put(T1 + i, sb[T1 + i].astype(F32) + got(XS + N2 + i) + got(T2 + i))
            put(T1 + j, sb[T1 + j].astype(F32) + got(XS + N2 + j))
            put(T3 + i, sb[T3 + i].astype(F32) + got(XS + 3 * N2 + i))
            put(T3 + j, sb[T3 + j].astype(F32) + got(XS + 3 * N2 + j) + got(T2 + j))

        each(H2, body)
        t1.start()
        t3.start()

        def write(r, value):
            out_ref[r] = value.astype(BF)

        def flush(i, start, count):
            return pltpu.make_async_copy(out_ref.at[pl.ds(start, count)], out_hbm.at[pl.ds(start, count)], loc_sem.at[16 + i])

        flushes = [flush(0, N1, N2), flush(1, 0, H1), flush(2, H1, H1)]

        xs0.wait_recv()
        t1.wait_recv()
        t3.wait_recv()

        def body(i):
            write(N1 + i, pick(N1 + i)[0] + got(XS + i) + got(T1 + i) + got(T3 + i))

        each(N2, body)
        flushes[0].start()
        m2p.wait_recv()
        m2m.wait_recv()
        for start, copy, copy_out in ((0, xfa, flushes[1]), (H1, xfb, flushes[2])):
            copy.wait_recv()

            def body(i):
                j = start + i
                write(j, pick(j)[0] + got(M2P + j) + got(M2M + j) + got(XF + j))

            each(H1, body)
            copy_out.start()
        for copy in messages:
            copy.wait_send()
        for copy_out in flushes:
            copy_out.wait()

    for copy in w2_copies + late:
        copy.wait()
    pl.run_scoped(
        layer_two,
        pltpu.VMEM((NA, 4 * TILE, 1024), BF),
        pltpu.VMEM((64, TILE, 4 * TILE), BF),
        pltpu.VMEM((PAIRS + 1, TILE, 2 * TILE), BF),
        pltpu.VMEM((TILE, 2 * TILE), F32),
    )


def on_device(features, tile_values, tile_row, tile_col, weight_one, bias_one, weight_two):
    hbm = pl.BlockSpec(memory_space=pl.ANY)
    dma = pltpu.SemaphoreType.DMA
    return pl.pallas_call(
        kernel,
        out_shape=jax.ShapeDtypeStruct((RB, TILE, TILE), BF),
        in_specs=[hbm] * 7,
        out_specs=hbm,
        scratch_shapes=[
            pltpu.VMEM((129, TILE, TILE), BF),
            pltpu.VMEM((NB, 1024, TILE), BF),
            pltpu.VMEM((64, TILE, TILE), BF),
            pltpu.VMEM((C_BLOCKS, TILE, TILE), F32),
            pltpu.VMEM((64, TILE, TILE), BF),
            pltpu.VMEM((BLOCKS, TILE, TILE), BF),
            pltpu.VMEM((BLOCKS, TILE, TILE), BF),
            pltpu.VMEM((8, 2 * TILE), jnp.int32),
            pltpu.VMEM((8, TILE), F32),
            pltpu.SMEM((8, 2 * TILE), jnp.int32),
            pltpu.SMEM((8, TILE), F32),
            pltpu.VMEM((1, TILE), jnp.int32),
            pltpu.VMEM((1, TILE), jnp.int32),
            pltpu.VMEM((TILE, 1024), BF),
            pltpu.VMEM((1, 1024), F32),
            pltpu.VMEM((RB, TILE, TILE), BF),
        ]
        + [dma((19,))]
        + [dma((12,))] * 4
        + [dma((15,))] * 2
        + [dma((12,))] * 4
        + [dma((18,))] * 2,
        compiler_params=pltpu.CompilerParams(
            collective_id=0, has_side_effects=True, vmem_limit_bytes=64 * 2**20 - 2**16
        ),
        cost_estimate=pl.CostEstimate(flops=26 * 10**9, bytes_accessed=8 * 2**20, transcendentals=0),
        name="two_layers",
    )(tile_row.reshape(1, -1), tile_col.reshape(1, -1), features.reshape(4, TILE, TILE), tile_values, weight_one, bias_one.reshape(1, -1), weight_two).reshape(RB * TILE, TILE)


def solution(mesh):
    return jax.shard_map(
        on_device,
        mesh=mesh,
        in_specs=(
            P(("aa", "ba"), None),
            P(("aa", "ba"), None, None),
            P(("aa", "ba")),
            P(("aa", "ba")),
            P(),
            P(),
            P(),
        ),
        out_specs=P("aa", "ba"),
        check_vma=False,
    )
```

```python
import functools

import jax
import jax.numpy as jnp
from jax import lax
from jax.experimental import pallas as pl
from jax.experimental.pallas import tpu as pltpu
from jax.sharding import PartitionSpec as P

MESH = pl.DeviceIdType.MESH
TILE = 128
NZ = 4
NB = 8
NA = 16
RB = 32
N1 = 18
H1 = N1 // 2
X1 = 12
N2 = RB - N1
H2 = N2 // 2
M0P, M0M, M1P, M1M, M2P, M2M = 0, N1, 2 * N1, 3 * N1, 4 * N1, 5 * N1
XS = 6 * N1
T2 = XS + 4 * N2
T1 = T2 + N2
T3 = T1 + N2
XF = T3 + N2
BLOCKS = XF + N1
PAIRS = 80
BF = jnp.bfloat16
F32 = jnp.float32
C_M0P, C_M0M, C_M1P, C_M1M, C_XS, C_T2, C_T1, C_T3, C_XF, C_BLOCKS = 0, 2, 4, 8, 12, 20, 22, 24, 26, 28


def prepare(tile_row, tile_col, index_v, keep_v):
    slots = TILE
    square = (slots, slots)

    def iota(dim, shape=square):
        return lax.broadcasted_iota(jnp.int32, shape, dim)

    def over_rows(x):
        return jnp.sum(x, axis=0, keepdims=True)

    def over_lanes(x):
        return jnp.sum(x, axis=1, keepdims=True)

    row_l = jnp.broadcast_to(jnp.where(tile_row < 0, -1, tile_row & (RB - 1)), square)
    clamped = jnp.maximum(tile_col, 0)
    col_l = jnp.broadcast_to((clamped >> 5) * 4 + (clamped & 3), square)
    row_s, col_s = row_l.T, col_l.T
    down, across = iota(0), iota(1)
    zero, one = jnp.zeros(square, jnp.int32), jnp.ones(square, jnp.int32)

    hot = row_s == across
    count_l = over_rows(jnp.where(hot, one, zero))
    count_s = over_lanes(jnp.where(row_l == down, one, zero))
    pairs_l, pairs_s = (count_l + 1) >> 1, (count_s + 1) >> 1
    start_l = over_rows(jnp.where(down < across, pairs_s, zero))
    start_s = over_lanes(jnp.where(across < down, pairs_l, zero))
    rank_s = over_lanes(jnp.where((row_l == row_s) & (across < down), one, zero))
    slot_start = over_lanes(jnp.where(hot, start_l, zero))
    place = jnp.where(row_s[:, :1] >= 0, 2 * slot_start + rank_s, -1)
    wide = (slots, 2 * TILE)
    match = place == iota(1, wide)
    nothing = jnp.zeros(wide, jnp.int32)
    slot_at = slots + over_rows(jnp.where(match, iota(0, wide) - slots, nothing))
    col_at = over_rows(jnp.where(match, col_s[:, :1], nothing))
    inside = (across > start_s) & (across < start_s + pairs_s)
    last = jnp.where(count_l > 0, start_l + pairs_l - 1, PAIRS)
    index_v[...] = jnp.zeros(index_v.shape, jnp.int32)
    index_v[0:1, :] = slot_at
    index_v[1:2, :] = col_at
    index_v[2:3, 0:TILE] = last
    keep_v[0:1, :] = over_rows(jnp.where(inside, one, zero)).astype(F32)


def kernel(
    row_hbm, col_hbm, x_hbm, tiles_hbm, w1_hbm, b1_hbm, w2_hbm, out_hbm,
    tiles, w2c, feats, cr, lows, sb, rb, index_v, keep_v, index, keeps, row_ref, col_ref, w1_ref, b1_ref, out_ref,
    loc_sem, as_sem, ar_sem, fs_sem, fr_sem, cs_sem, cr_sem, ds_sem, dr_sem, gs_sem, gr_sem, es_sem, er_sem,
):
    a, b = lax.axis_index("aa"), lax.axis_index("ba")
    y, xh, c = a // 4, lax.rem(a // 2, 2), lax.rem(a, 2)
    xl, z = b // NZ, lax.rem(b, NZ)

    def aa_of(dy, dx):
        return lax.rem(y + dy, 4) * 4 + lax.rem(xh + dx, 2) * 2 + c

    def ba_of(dx, dz):
        return lax.rem(xl + dx, 2) * NZ + lax.rem(z + dz, NZ)

    sibling = (a + 1 - 2 * c, b)
    zp, zm = (a, ba_of(0, 1)), (a, ba_of(0, 3))
    xn = (a, ba_of(1, 0))

    barrier = pltpu.get_barrier_semaphore()
    for k in (4, 1, 2, 6):
        pl.semaphore_signal(barrier, inc=1, device_id=(aa_of(k // 2, k % 2), b), device_id_type=MESH)
    for peer in (sibling, zp, zm, xn):
        pl.semaphore_signal(barrier, inc=1, device_id=peer, device_id_type=MESH)

    early = [
        pltpu.make_async_copy(x_hbm, feats.at[pl.ds(a * 4, 4)], loc_sem.at[11]),
        pltpu.make_async_copy(row_hbm, row_ref, loc_sem.at[12]),
        pltpu.make_async_copy(col_hbm, col_ref, loc_sem.at[13]),
    ]
    late = [
        pltpu.make_async_copy(w1_hbm, w1_ref, loc_sem.at[14]),
        pltpu.make_async_copy(b1_hbm, b1_ref, loc_sem.at[15]),
    ]
    for copy in early + late:
        copy.start()
    tile_copy = pltpu.make_async_copy(tiles_hbm, tiles.at[pl.ds(0, 128)], loc_sem.at[0])
    tile_copy.start()
    w2_copies = []
    for f in range(NB):
        w2_copies.append(
            pltpu.make_async_copy(
                w2_hbm.at[:, pl.ds(f * TILE, TILE)],
                w2c.at[f],
                loc_sem.at[1 + f],
            )
        )
        w2_copies[-1].start()

    tiles[128] = jnp.zeros((TILE, TILE), BF)

    early[0].wait()
    pl.semaphore_wait(barrier, 8)

    def gather(buf, s_sem, r_sem, s_fwd, r_fwd, use, between=None):
        def block(owner):
            return buf.at[pl.ds(owner * 4, 4)]

        def remote(i, ref, peer):
            return pltpu.make_async_remote_copy(
                src_ref=ref, dst_ref=ref, send_sem=s_sem.at[i], recv_sem=r_sem.at[i],
                device_id=(peer, b), device_id_type=MESH,
            )

        def to_peer(k):
            return remote(k, block(a), aa_of(k // 2, k % 2))

        def first_half(dy):
            return remote(2 * dy + 1, buf.at[pl.ds(aa_of(0, 1) * 4, 2)], aa_of(dy, 0))

        def second_half(dy):
            return remote(8 + dy, buf.at[pl.ds(aa_of(4 - dy, 0) * 4 + 2, 2)], aa_of(0, 1))

        def forward(k):
            owner = aa_of(4 - k // 2, lax.rem(k, 2))
            return pltpu.make_async_remote_copy(
                src_ref=block(owner), dst_ref=block(owner), send_sem=s_fwd.at[k], recv_sem=r_fwd.at[k],
                device_id=sibling, device_id_type=MESH,
            )

        for k in (1, 6, 2, 4):
            to_peer(k).start()
        forward(0).start()

        if between is not None:
            between()

        def own(k, l):
            if use is not None:
                use(aa_of(4 - k // 2, k % 2), aa_of(4 - l // 2, l % 2))

        def other(k, l):
            forward(k).wait_recv()
            forward(l).wait_recv()
            if use is not None:
                use(aa_of(4 - k // 2, k % 2) + 1 - 2 * c, aa_of(4 - l // 2, l % 2) + 1 - 2 * c)

        to_peer(1).wait_recv()
        for dy in (2, 1, 3):
            first_half(dy).start()
        forward(1).start()
        own(0, 1)
        for dy in (1, 3):
            to_peer(2 * dy).wait_recv()
            second_half(dy).start()
            forward(2 * dy).start()
        own(2, 6)
        to_peer(4).wait_recv()
        second_half(2).start()
        forward(4).start()
        other(0, 1)
        other(2, 6)
        for dy in (1, 3):
            first_half(dy).wait_recv()
            second_half(dy).wait_recv()
            forward(2 * dy + 1).start()
        own(4, 3)
        first_half(2).wait_recv()
        second_half(2).wait_recv()
        forward(5).start()
        own(7, 5)
        other(4, 3)
        other(7, 5)

        def finish():
            for k in (1, 2, 4, 6):
                to_peer(k).wait_send()
            for dy in (1, 2, 3):
                first_half(dy).wait_send()
                second_half(dy).wait_send()
            for k in range(8):
                forward(k).wait_send()

        return finish

    index_copy = pltpu.make_async_copy(index_v, index, loc_sem.at[9])
    keep_copy = pltpu.make_async_copy(keep_v, keeps, loc_sem.at[10])

    def order():
        early[1].wait()
        early[2].wait()
        prepare(row_ref[...], col_ref[...], index_v, keep_v)
        index_copy.start()
        keep_copy.start()

    finish_a = gather(feats, as_sem, ar_sem, fs_sem, fr_sem, None, order)
    tile_copy.wait()
    index_copy.wait()
    keep_copy.wait()

    group = 20

    def pair_products(source, offset, width, acc, store):
        acc[:, pl.ds(0, width)] = jnp.zeros((TILE, width), F32)

        def body(i, carry):
            running = acc[:, pl.ds(0, width)]
            for j in range(group):
                q = i * group + j
                left = jnp.concatenate([tiles[index[0, 2 * q]], tiles[index[0, 2 * q + 1]]], axis=1)
                cols = pl.ds(offset, width)
                right = jnp.concatenate([source[index[1, 2 * q], :, cols], source[index[1, 2 * q + 1], :, cols]], axis=0)
                running = running * keeps[0, q] + jnp.dot(left, right, preferred_element_type=F32)
                store(q, running)
            acc[:, pl.ds(0, width)] = running
            return carry

        lax.fori_loop(0, PAIRS // group, body, 0)

    def each(count, body):
        def one(i, carry):
            body(i)
            return carry

        lax.fori_loop(0, count, one, 0)

    def layer_one(sums1, acc, cs):
        sums1[PAIRS] = jnp.zeros((TILE, TILE), F32)

        def store1(q, value):
            sums1[q] = value

        pair_products(feats, 0, TILE, acc, store1)

        def own(dx, dz, j):
            return sums1[index[2, ba_of(dx, dz) * 4 + j]]

        def message(i, offset, count, peer):
            return pltpu.make_async_remote_copy(
                src_ref=cs.at[pl.ds(offset, count)], dst_ref=cr.at[pl.ds(offset, count)],
                send_sem=cs_sem.at[i], recv_sem=cr_sem.at[i], device_id=peer, device_id_type=MESH,
            )

        m0p, m0m = message(0, C_M0P, 2, zp), message(1, C_M0M, 2, zm)
        xsa, xsb = message(2, C_XS, 2, xn), message(3, C_XS + 2, 6, xn)
        m1pb, m1ma = message(4, C_M1P + 2, 2, zp), message(5, C_M1M, 2, zm)
        m1pa, m1mb = message(6, C_M1P, 2, zp), message(7, C_M1M + 2, 2, zm)
        t2p, t2m = message(8, C_T2, 1, zp), message(9, C_T2 + 1, 1, zm)
        t1b, t3a = message(10, C_T1 + 1, 1, zp), message(11, C_T3, 1, zm)
        t1a, t3b = message(12, C_T1, 1, zp), message(13, C_T3 + 1, 1, zm)
        xf = message(14, C_XF, 2, xn)

        for dx in range(2):
            cs[C_M0P + dx] = own(dx, 2, 0)
            cs[C_M0M + dx] = own(dx, 2, 1)
        m0p.start()
        m0m.start()
        for j in range(2):
            cs[C_XS + j] = own(1, 2, 2 + j)
        xsa.start()
        for j in range(2):
            cs[C_XS + 2 + j] = own(1, 1, 2 + j)
            cs[C_XS + 4 + j] = own(1, 3, 2 + j)
            cs[C_XS + 6 + j] = own(1, 0, 2 + j)
        xsb.start()
        for dx in range(2):
            cs[C_M1P + 2 + dx] = own(dx, 1, 1)
            cs[C_M1M + dx] = own(dx, 3, 0)
        m1pb.start()
        m1ma.start()
        xsa.wait_recv()
        for j in range(2):
            cs[C_T2 + j] = own(0, 2, 2 + j) + cr[C_XS + j]
        t2p.start()
        t2m.start()
        m0p.wait_recv()
        m0m.wait_recv()
        for dx in range(2):
            cs[C_M1P + dx] = own(dx, 1, 0) + cr[C_M0P + dx]
            cs[C_M1M + 2 + dx] = own(dx, 3, 1) + cr[C_M0M + dx]
        m1pa.start()
        m1mb.start()
        xsb.wait_recv()
        cs[C_T1 + 1] = own(0, 1, 3) + cr[C_XS + 3]
        cs[C_T3] = own(0, 3, 2) + cr[C_XS + 4]
        t1b.start()
        t3a.start()
        t2p.wait_recv()
        t2m.wait_recv()
        cs[C_T1] = own(0, 1, 2) + cr[C_XS + 2] + cr[C_T2]
        cs[C_T3 + 1] = own(0, 3, 3) + cr[C_XS + 5] + cr[C_T2 + 1]
        t1a.start()
        t3b.start()
        for copy in (m1pb, m1ma, m1pa, m1mb):
            copy.wait_recv()
        for j in range(2):
            cs[C_XF + j] = own(1, 0, j) + cr[C_M1P + 2 * j + 1] + cr[C_M1M + 2 * j + 1]
        xf.start()
        for copy in (t1b, t3a, t1a, t3b):
            copy.wait_recv()
        for j in range(2):
            value = own(0, 0, 2 + j) + cr[C_XS + 6 + j] + cr[C_T1 + j] + cr[C_T3 + j]
            lows[a * 4 + 2 + j] = value.astype(BF)
        xf.wait_recv()
        for j in range(2):
            value = own(0, 0, j) + cr[C_M1P + 2 * j] + cr[C_M1M + 2 * j] + cr[C_XF + j]
            lows[a * 4 + j] = value.astype(BF)
        for copy in (m0p, m0m, xsa, xsb, m1pb, m1ma, m1pa, m1mb, t2p, t2m, t1b, t3a, t1a, t3b, xf):
            copy.wait_send()

    pl.run_scoped(
        layer_one,
        pltpu.VMEM((PAIRS + 1, TILE, TILE), F32),
        pltpu.VMEM((TILE, TILE), F32),
        pltpu.VMEM((C_BLOCKS, TILE, TILE), F32),
    )
    finish_a()


    def message(i, offset, count, peer):
        return pltpu.make_async_remote_copy(
            src_ref=sb.at[pl.ds(offset, count)], dst_ref=rb.at[pl.ds(offset, count)],
            send_sem=es_sem.at[i], recv_sem=er_sem.at[i], device_id=peer, device_id_type=MESH,
        )

    m0p, m0m = message(0, M0P, N1, zp), message(1, M0M, N1, zm)
    xs2 = message(2, XS + 2 * N2, N2, xn)
    m1pb, m1ma = message(3, M1P + H1, H1, zp), message(4, M1M, H1, zm)
    xs1, xs3 = message(5, XS + N2, N2, xn), message(6, XS + 3 * N2, N2, xn)
    t2p, t2m = message(7, T2, H2, zp), message(8, T2 + H2, H2, zm)
    m1pa, m1mb = message(9, M1P, H1, zp), message(10, M1M + H1, H1, zm)
    m2p, m2m = message(11, M2P, N1, zp), message(12, M2M, N1, zm)
    t1, t3 = message(13, T1, N2, zp), message(14, T3, N2, zm)
    xs0 = message(15, XS, N2, xn)
    xfa, xfb = message(16, XF, X1, xn), message(17, XF + X1, N1 - X1, xn)
    messages = [m0p, m0m, xs2, m1pb, m1ma, xs1, xs3, t2p, t2m, m1pa, m1mb, m2p, m2m, t1, t3, xs0, xfa, xfb]

    def layer_two(hid, proj, sums2, acc):
        sums2[PAIRS] = jnp.zeros((TILE, 2 * TILE), BF)

        def columns(s):
            places = (((0, 2), (1, 2)), ((1, 1), (1, 3)), ((0, 1), (0, 3)), ((0, 0), (1, 0)))[s]
            return jnp.concatenate([w2c[ba_of(dx, dz)] for dx, dz in places], axis=1)

        def project(rows, s):
            return jnp.dot(rows, columns(s), preferred_element_type=F32).astype(BF)

        def project_all(s):
            def body(i):
                rows = hid[pl.ds(4 * i, 4)].reshape(16 * TILE, 1024)
                value = project(rows, s).reshape(16, TILE, 2 * TILE)
                proj[pl.ds(16 * i, 16), :, pl.ds(s % 2 * 2 * TILE, 2 * TILE)] = value

            each(NA // 4, body)

        def hidden_of(one, two):
            rows = [lows[pl.ds(o * 4, 4)].reshape(4 * TILE, TILE) for o in (one, two)]
            value = jnp.dot(jnp.concatenate(rows, axis=0), w1_ref[...], preferred_element_type=F32) + b1_ref[...]
            value = jnp.maximum(value, 0.0).astype(BF)
            hid[one] = value[: 4 * TILE]
            hid[two] = value[4 * TILE :]
            value = project(value, 0).reshape(8, TILE, 2 * TILE)
            proj[pl.ds(one * 4, 4), :, pl.ds(0, 2 * TILE)] = value[:4]
            proj[pl.ds(two * 4, 4), :, pl.ds(0, 2 * TILE)] = value[4:]

        finish_d = gather(lows, ds_sem, dr_sem, gs_sem, gr_sem, hidden_of)
        finish_d()

        def store2(q, value):
            sums2[q] = value.astype(BF)

        def pick(r):
            value = sums2[index[2, r]].astype(F32)
            return value[:, :TILE], value[:, TILE:]

        def got(i):
            return rb[i].astype(F32)

        def put(i, value):
            sb[i] = value.astype(BF)

        pair_products(proj, 0 * TILE, 2 * TILE, acc, store2)

        def body(i):
            near, far = pick(i)
            put(M0P + i, near)
            put(M0P + H1 + i, far)
            near, far = pick(H1 + i)
            put(M0M + i, near)
            put(M0M + H1 + i, far)

        each(H1, body)
        m0p.start()
        m0m.start()

        def body(i):
            near, far = pick(N1 + i)
            put(T2 + i, near)
            put(XS + 2 * N2 + i, far)

        each(N2, body)
        xs2.start()

        project_all(1)

        pair_products(proj, 2 * TILE, 2 * TILE, acc, store2)

        def body(i):
            plus, minus = pick(N1 + i)
            put(XS + N2 + i, plus)
            put(XS + 3 * N2 + i, minus)

        each(N2, body)
        xs1.start()
        xs3.start()

        def body(i):
            put(M1M + i, pick(i)[1])
            put(M1P + H1 + i, pick(H1 + i)[0])

        each(H1, body)
        m1pb.start()
        m1ma.start()

        project_all(2)
        m0p.wait_recv()
        m0m.wait_recv()

        def body(i):
            put(M1P + i, pick(i)[0] + got(M0P + H1 + i))
            put(M1M + H1 + i, pick(H1 + i)[1] + got(M0M + H1 + i))

        each(H1, body)
        m1pa.start()
        m1mb.start()
        xs2.wait_recv()

        def body(i):
            put(T2 + i, sb[T2 + i].astype(F32) + got(XS + 2 * N2 + i))

        each(N2, body)
        t2p.start()
        t2m.start()

        pair_products(proj, 0 * TILE, 2 * TILE, acc, store2)

        def body(i):
            plus, minus = pick(i)
            put(M2P + i, plus + got(M0P + i))
            put(M2M + i, minus)
            plus, minus = pick(H1 + i)
            put(M2P + H1 + i, plus)
            put(M2M + H1 + i, minus + got(M0M + i))

        each(H1, body)
        m2p.start()
        m2m.start()

        def body(i):
            plus, minus = pick(N1 + i)
            put(T1 + i, plus)
            put(T3 + i, minus)

        each(N2, body)
        project_all(3)

        pair_products(proj, 2 * TILE, 2 * TILE, acc, store2)

        def body(i):
            put(XS + i, pick(N1 + i)[1])

        each(N2, body)
        xs0.start()
        m1pb.wait_recv()
        m1ma.wait_recv()
        m1pa.wait_recv()
        m1mb.wait_recv()

        def body(i):
            put(XF + i, pick(i)[1] + got(M1P + i) + got(M1M + i))

        each(X1, body)
        xfa.start()

        def body(i):
            j = X1 + i
            put(XF + j, pick(j)[1] + got(M1P + j) + got(M1M + j))

        each(N1 - X1, body)
        xfb.start()

        for copy in (xs1, xs3, t2p, t2m):
            copy.wait_recv()

        def body(i):
            j = H2 + i
            put(T1 + i, sb[T1 + i].astype(F32) + got(XS + N2 + i) + got(T2 + i))
            put(T1 + j, sb[T1 + j].astype(F32) + got(XS + N2 + j))
            put(T3 + i, sb[T3 + i].astype(F32) + got(XS + 3 * N2 + i))
            put(T3 + j, sb[T3 + j].astype(F32) + got(XS + 3 * N2 + j) + got(T2 + j))

        each(H2, body)
        t1.start()
        t3.start()

        def write(r, value):
            out_ref[r] = value.astype(BF)

        def flush(i, start, count):
            return pltpu.make_async_copy(out_ref.at[pl.ds(start, count)], out_hbm.at[pl.ds(start, count)], loc_sem.at[16 + i])

        flushes = [flush(0, N1, N2), flush(1, 0, X1), flush(2, X1, N1 - X1)]

        xs0.wait_recv()
        t1.wait_recv()
        t3.wait_recv()

        def body(i):
            write(N1 + i, pick(N1 + i)[0] + got(XS + i) + got(T1 + i) + got(T3 + i))

        each(N2, body)
        flushes[0].start()
        m2p.wait_recv()
        m2m.wait_recv()
        for start, count, copy, copy_out in ((0, X1, xfa, flushes[1]), (X1, N1 - X1, xfb, flushes[2])):
            copy.wait_recv()

            def body(i):
                j = start + i
                write(j, pick(j)[0] + got(M2P + j) + got(M2M + j) + got(XF + j))

            each(count, body)
            copy_out.start()
        for copy in messages:
            copy.wait_send()
        for copy_out in flushes:
            copy_out.wait()

    for copy in w2_copies + late:
        copy.wait()
    pl.run_scoped(
        layer_two,
        pltpu.VMEM((NA, 4 * TILE, 1024), BF),
        pltpu.VMEM((64, TILE, 4 * TILE), BF),
        pltpu.VMEM((PAIRS + 1, TILE, 2 * TILE), BF),
        pltpu.VMEM((TILE, 2 * TILE), F32),
    )


def on_device(features, tile_values, tile_row, tile_col, weight_one, bias_one, weight_two):
    hbm = pl.BlockSpec(memory_space=pl.ANY)
    dma = pltpu.SemaphoreType.DMA
    return pl.pallas_call(
        kernel,
        out_shape=jax.ShapeDtypeStruct((RB, TILE, TILE), BF),
        in_specs=[hbm] * 7,
        out_specs=hbm,
        scratch_shapes=[
            pltpu.VMEM((129, TILE, TILE), BF),
            pltpu.VMEM((NB, 1024, TILE), BF),
            pltpu.VMEM((64, TILE, TILE), BF),
            pltpu.VMEM((C_BLOCKS, TILE, TILE), F32),
            pltpu.VMEM((64, TILE, TILE), BF),
            pltpu.VMEM((BLOCKS, TILE, TILE), BF),
            pltpu.VMEM((BLOCKS, TILE, TILE), BF),
            pltpu.VMEM((8, 2 * TILE), jnp.int32),
            pltpu.VMEM((8, TILE), F32),
            pltpu.SMEM((8, 2 * TILE), jnp.int32),
            pltpu.SMEM((8, TILE), F32),
            pltpu.VMEM((1, TILE), jnp.int32),
            pltpu.VMEM((1, TILE), jnp.int32),
            pltpu.VMEM((TILE, 1024), BF),
            pltpu.VMEM((1, 1024), F32),
            pltpu.VMEM((RB, TILE, TILE), BF),
        ]
        + [dma((19,))]
        + [dma((12,))] * 4
        + [dma((15,))] * 2
        + [dma((12,))] * 4
        + [dma((18,))] * 2,
        compiler_params=pltpu.CompilerParams(
            collective_id=0, has_side_effects=True, vmem_limit_bytes=64 * 2**20 - 2**16
        ),
        cost_estimate=pl.CostEstimate(flops=26 * 10**9, bytes_accessed=8 * 2**20, transcendentals=0),
        name="two_layers",
    )(tile_row.reshape(1, -1), tile_col.reshape(1, -1), features.reshape(4, TILE, TILE), tile_values, weight_one, bias_one.reshape(1, -1), weight_two).reshape(RB * TILE, TILE)


def solution(mesh):
    return jax.shard_map(
        on_device,
        mesh=mesh,
        in_specs=(
            P(("aa", "ba"), None),
            P(("aa", "ba"), None, None),
            P(("aa", "ba")),
            P(("aa", "ba")),
            P(),
            P(),
            P(),
        ),
        out_specs=P("aa", "ba"),
        check_vma=False,
    )
```

```python
import functools

import jax
import jax.numpy as jnp
from jax import lax
from jax.experimental import pallas as pl
from jax.experimental.pallas import tpu as pltpu
from jax.sharding import PartitionSpec as P

MESH = pl.DeviceIdType.MESH
TILE = 128
NZ = 4
NB = 8
NA = 16
RB = 32
N1 = 18
H1 = N1 // 2
X1 = 12
N2 = RB - N1
H2 = N2 // 2
M0P, M0M, M1P, M1M, M2P, M2M = 0, N1, 2 * N1, 3 * N1, 4 * N1, 5 * N1
XS = 6 * N1
T2 = XS + 4 * N2
T1 = T2 + N2
T3 = T1 + N2
XF = T3 + N2
BLOCKS = XF + N1
PAIRS = 80
BF = jnp.bfloat16
F32 = jnp.float32
C_M0P, C_M0M, C_M1P, C_M1M, C_XS, C_T2, C_T1, C_T3, C_XF, C_BLOCKS = 0, 2, 4, 8, 12, 20, 22, 24, 26, 28


def prepare(tile_row, tile_col, index_v, keep_v):
    slots = TILE
    square = (slots, slots)

    def iota(dim, shape=square):
        return lax.broadcasted_iota(jnp.int32, shape, dim)

    def over_rows(x):
        return jnp.sum(x, axis=0, keepdims=True)

    def over_lanes(x):
        return jnp.sum(x, axis=1, keepdims=True)

    row_l = jnp.broadcast_to(jnp.where(tile_row < 0, -1, tile_row & (RB - 1)), square)
    clamped = jnp.maximum(tile_col, 0)
    col_l = jnp.broadcast_to((clamped >> 5) * 4 + (clamped & 3), square)
    row_s, col_s = row_l.T, col_l.T
    down, across = iota(0), iota(1)
    zero, one = jnp.zeros(square, jnp.int32), jnp.ones(square, jnp.int32)

    hot = row_s == across
    count_l = over_rows(jnp.where(hot, one, zero))
    count_s = over_lanes(jnp.where(row_l == down, one, zero))
    pairs_l, pairs_s = (count_l + 1) >> 1, (count_s + 1) >> 1
    start_l = over_rows(jnp.where(down < across, pairs_s, zero))
    start_s = over_lanes(jnp.where(across < down, pairs_l, zero))
    rank_s = over_lanes(jnp.where((row_l == row_s) & (across < down), one, zero))
    slot_start = over_lanes(jnp.where(hot, start_l, zero))
    place = jnp.where(row_s[:, :1] >= 0, 2 * slot_start + rank_s, -1)
    wide = (slots, 2 * TILE)
    match = place == iota(1, wide)
    nothing = jnp.zeros(wide, jnp.int32)
    slot_at = slots + over_rows(jnp.where(match, iota(0, wide) - slots, nothing))
    col_at = over_rows(jnp.where(match, col_s[:, :1], nothing))
    inside = (across > start_s) & (across < start_s + pairs_s)
    last = jnp.where(count_l > 0, start_l + pairs_l - 1, PAIRS)
    index_v[...] = jnp.zeros(index_v.shape, jnp.int32)
    index_v[0:1, :] = slot_at
    index_v[1:2, :] = col_at
    index_v[2:3, 0:TILE] = last
    keep_v[0:1, :] = over_rows(jnp.where(inside, one, zero)).astype(F32)


def kernel(
    row_hbm, col_hbm, x_hbm, tiles_hbm, w1_hbm, b1_hbm, w2_hbm, out_hbm,
    tiles, w2c, feats, cr, lows, sb, rb, index_v, keep_v, index, keeps, row_ref, col_ref, w1_ref, b1_ref, out_ref,
    loc_sem, as_sem, ar_sem, fs_sem, fr_sem, cs_sem, cr_sem, ds_sem, dr_sem, gs_sem, gr_sem, es_sem, er_sem,
):
    a, b = lax.axis_index("aa"), lax.axis_index("ba")
    y, xh, c = a // 4, lax.rem(a // 2, 2), lax.rem(a, 2)
    xl, z = b // NZ, lax.rem(b, NZ)

    def aa_of(dy, dx):
        return lax.rem(y + dy, 4) * 4 + lax.rem(xh + dx, 2) * 2 + c

    def ba_of(dx, dz):
        return lax.rem(xl + dx, 2) * NZ + lax.rem(z + dz, NZ)

    sibling = (a + 1 - 2 * c, b)
    zp, zm = (a, ba_of(0, 1)), (a, ba_of(0, 3))
    xn = (a, ba_of(1, 0))

    barrier = pltpu.get_barrier_semaphore()
    for k in (4, 1, 2, 6):
        pl.semaphore_signal(barrier, inc=1, device_id=(aa_of(k // 2, k % 2), b), device_id_type=MESH)
    for peer in (sibling, zp, zm, xn):
        pl.semaphore_signal(barrier, inc=1, device_id=peer, device_id_type=MESH)

    early = [
        pltpu.make_async_copy(x_hbm, feats.at[pl.ds(a * 4, 4)], loc_sem.at[11]),
        pltpu.make_async_copy(row_hbm, row_ref, loc_sem.at[12]),
        pltpu.make_async_copy(col_hbm, col_ref, loc_sem.at[13]),
    ]
    late = [
        pltpu.make_async_copy(w1_hbm, w1_ref, loc_sem.at[14]),
        pltpu.make_async_copy(b1_hbm, b1_ref, loc_sem.at[15]),
    ]
    for copy in early + late:
        copy.start()
    tile_copy = pltpu.make_async_copy(tiles_hbm, tiles.at[pl.ds(0, 128)], loc_sem.at[0])
    tile_copy.start()
    w2_copies = []
    for f in range(NB):
        w2_copies.append(
            pltpu.make_async_copy(
                w2_hbm.at[:, pl.ds(f * TILE, TILE)],
                w2c.at[f],
                loc_sem.at[1 + f],
            )
        )
        w2_copies[-1].start()

    tiles[128] = jnp.zeros((TILE, TILE), BF)

    early[0].wait()
    pl.semaphore_wait(barrier, 8)

    def gather(buf, s_sem, r_sem, s_fwd, r_fwd, use, between=None):
        def block(owner):
            return buf.at[pl.ds(owner * 4, 4)]

        def remote(i, ref, peer):
            return pltpu.make_async_remote_copy(
                src_ref=ref, dst_ref=ref, send_sem=s_sem.at[i], recv_sem=r_sem.at[i],
                device_id=(peer, b), device_id_type=MESH,
            )

        def to_peer(k):
            return remote(k, block(a), aa_of(k // 2, k % 2))

        def first_half(dy):
            return remote(2 * dy + 1, buf.at[pl.ds(aa_of(0, 1) * 4, 2)], aa_of(dy, 0))

        def second_half(dy):
            return remote(8 + dy, buf.at[pl.ds(aa_of(4 - dy, 0) * 4 + 2, 2)], aa_of(0, 1))

        def forward(k):
            owner = aa_of(4 - k // 2, lax.rem(k, 2))
            return pltpu.make_async_remote_copy(
                src_ref=block(owner), dst_ref=block(owner), send_sem=s_fwd.at[k], recv_sem=r_fwd.at[k],
                device_id=sibling, device_id_type=MESH,
            )

        for k in (1, 6, 2, 4):
            to_peer(k).start()
        forward(0).start()

        if between is not None:
            between()

        def own(k, l):
            if use is not None:
                use(aa_of(4 - k // 2, k % 2), aa_of(4 - l // 2, l % 2))

        def other(k, l):
            forward(k).wait_recv()
            forward(l).wait_recv()
            if use is not None:
                use(aa_of(4 - k // 2, k % 2) + 1 - 2 * c, aa_of(4 - l // 2, l % 2) + 1 - 2 * c)

        to_peer(1).wait_recv()
        for dy in (2, 1, 3):
            first_half(dy).start()
        forward(1).start()
        own(0, 1)
        for dy in (1, 3):
            to_peer(2 * dy).wait_recv()
            second_half(dy).start()
            forward(2 * dy).start()
        own(2, 6)
        to_peer(4).wait_recv()
        second_half(2).start()
        forward(4).start()
        other(0, 1)
        other(2, 6)
        for dy in (1, 3):
            first_half(dy).wait_recv()
            second_half(dy).wait_recv()
            forward(2 * dy + 1).start()
        own(4, 3)
        first_half(2).wait_recv()
        second_half(2).wait_recv()
        forward(5).start()
        own(7, 5)
        other(4, 3)
        other(7, 5)

        def finish():
            for k in (1, 2, 4, 6):
                to_peer(k).wait_send()
            for dy in (1, 2, 3):
                first_half(dy).wait_send()
                second_half(dy).wait_send()
            for k in range(8):
                forward(k).wait_send()

        return finish

    index_copy = pltpu.make_async_copy(index_v, index, loc_sem.at[9])
    keep_copy = pltpu.make_async_copy(keep_v, keeps, loc_sem.at[10])

    def order():
        early[1].wait()
        early[2].wait()
        prepare(row_ref[...], col_ref[...], index_v, keep_v)
        index_copy.start()
        keep_copy.start()

    finish_a = gather(feats, as_sem, ar_sem, fs_sem, fr_sem, None, order)
    tile_copy.wait()
    index_copy.wait()
    keep_copy.wait()

    group = 20

    def pair_products(source, offset, width, acc, store):
        acc[:, pl.ds(0, width)] = jnp.zeros((TILE, width), F32)

        def body(i, carry):
            running = acc[:, pl.ds(0, width)]
            for j in range(group):
                q = i * group + j
                left = jnp.concatenate([tiles[index[0, 2 * q]], tiles[index[0, 2 * q + 1]]], axis=1)
                cols = pl.ds(offset, width)
                right = jnp.concatenate([source[index[1, 2 * q], :, cols], source[index[1, 2 * q + 1], :, cols]], axis=0)
                running = running * keeps[0, q] + jnp.dot(left, right, preferred_element_type=F32)
                store(q, running)
            acc[:, pl.ds(0, width)] = running
            return carry

        lax.fori_loop(0, PAIRS // group, body, 0)

    def each(count, body):
        def one(i, carry):
            body(i)
            return carry

        lax.fori_loop(0, count, one, 0)

    def layer_one(sums1, acc, cs):
        sums1[PAIRS] = jnp.zeros((TILE, TILE), F32)

        def store1(q, value):
            sums1[q] = value

        pair_products(feats, 0, TILE, acc, store1)

        def own(dx, dz, j):
            return sums1[index[2, ba_of(dx, dz) * 4 + j]]

        def message(i, offset, count, peer):
            return pltpu.make_async_remote_copy(
                src_ref=cs.at[pl.ds(offset, count)], dst_ref=cr.at[pl.ds(offset, count)],
                send_sem=cs_sem.at[i], recv_sem=cr_sem.at[i], device_id=peer, device_id_type=MESH,
            )

        m0p, m0m = message(0, C_M0P, 2, zp), message(1, C_M0M, 2, zm)
        xsa, xsb = message(2, C_XS, 2, xn), message(3, C_XS + 2, 6, xn)
        m1pb, m1ma = message(4, C_M1P + 2, 2, zp), message(5, C_M1M, 2, zm)
        m1pa, m1mb = message(6, C_M1P, 2, zp), message(7, C_M1M + 2, 2, zm)
        t2p, t2m = message(8, C_T2, 1, zp), message(9, C_T2 + 1, 1, zm)
        t1b, t3a = message(10, C_T1 + 1, 1, zp), message(11, C_T3, 1, zm)
        t1a, t3b = message(12, C_T1, 1, zp), message(13, C_T3 + 1, 1, zm)
        xf = message(14, C_XF, 2, xn)

        for dx in range(2):
            cs[C_M0P + dx] = own(dx, 2, 0)
            cs[C_M0M + dx] = own(dx, 2, 1)
        m0p.start()
        m0m.start()
        for j in range(2):
            cs[C_XS + j] = own(1, 2, 2 + j)
        xsa.start()
        for j in range(2):
            cs[C_XS + 2 + j] = own(1, 1, 2 + j)
            cs[C_XS + 4 + j] = own(1, 3, 2 + j)
            cs[C_XS + 6 + j] = own(1, 0, 2 + j)
        xsb.start()
        for dx in range(2):
            cs[C_M1P + 2 + dx] = own(dx, 1, 1)
            cs[C_M1M + dx] = own(dx, 3, 0)
        m1pb.start()
        m1ma.start()
        xsa.wait_recv()
        for j in range(2):
            cs[C_T2 + j] = own(0, 2, 2 + j) + cr[C_XS + j]
        t2p.start()
        t2m.start()
        m0p.wait_recv()
        m0m.wait_recv()
        for dx in range(2):
            cs[C_M1P + dx] = own(dx, 1, 0) + cr[C_M0P + dx]
            cs[C_M1M + 2 + dx] = own(dx, 3, 1) + cr[C_M0M + dx]
        m1pa.start()
        m1mb.start()
        xsb.wait_recv()
        cs[C_T1 + 1] = own(0, 1, 3) + cr[C_XS + 3]
        cs[C_T3] = own(0, 3, 2) + cr[C_XS + 4]
        t1b.start()
        t3a.start()
        t2p.wait_recv()
        t2m.wait_recv()
        cs[C_T1] = own(0, 1, 2) + cr[C_XS + 2] + cr[C_T2]
        cs[C_T3 + 1] = own(0, 3, 3) + cr[C_XS + 5] + cr[C_T2 + 1]
        t1a.start()
        t3b.start()
        for copy in (m1pb, m1ma, m1pa, m1mb):
            copy.wait_recv()
        for j in range(2):
            cs[C_XF + j] = own(1, 0, j) + cr[C_M1P + 2 * j + 1] + cr[C_M1M + 2 * j + 1]
        xf.start()
        for copy in (t1b, t3a, t1a, t3b):
            copy.wait_recv()
        for j in range(2):
            value = own(0, 0, 2 + j) + cr[C_XS + 6 + j] + cr[C_T1 + j] + cr[C_T3 + j]
            lows[a * 4 + 2 + j] = value.astype(BF)
        xf.wait_recv()
        for j in range(2):
            value = own(0, 0, j) + cr[C_M1P + 2 * j] + cr[C_M1M + 2 * j] + cr[C_XF + j]
            lows[a * 4 + j] = value.astype(BF)
        for copy in (m0p, m0m, xsa, xsb, m1pb, m1ma, m1pa, m1mb, t2p, t2m, t1b, t3a, t1a, t3b, xf):
            copy.wait_send()

    pl.run_scoped(
        layer_one,
        pltpu.VMEM((PAIRS + 1, TILE, TILE), F32),
        pltpu.VMEM((TILE, TILE), F32),
        pltpu.VMEM((C_BLOCKS, TILE, TILE), F32),
    )
    finish_a()


    def message(i, offset, count, peer):
        return pltpu.make_async_remote_copy(
            src_ref=sb.at[pl.ds(offset, count)], dst_ref=rb.at[pl.ds(offset, count)],
            send_sem=es_sem.at[i], recv_sem=er_sem.at[i], device_id=peer, device_id_type=MESH,
        )

    m0p, m0m = message(0, M0P, N1, zp), message(1, M0M, N1, zm)
    xs2 = message(2, XS + 2 * N2, N2, xn)
    m1pb, m1ma = message(3, M1P + H1, H1, zp), message(4, M1M, H1, zm)
    xs1, xs3 = message(5, XS + N2, N2, xn), message(6, XS + 3 * N2, N2, xn)
    t2p, t2m = message(7, T2, H2, zp), message(8, T2 + H2, H2, zm)
    m1pa, m1mb = message(9, M1P, H1, zp), message(10, M1M + H1, H1, zm)
    m2p, m2m = message(11, M2P, N1, zp), message(12, M2M, N1, zm)
    t1, t3 = message(13, T1, N2, zp), message(14, T3, N2, zm)
    xs0 = message(15, XS, N2, xn)
    xfa, xfb = message(16, XF, X1, xn), message(17, XF + X1, N1 - X1, xn)
    messages = [m0p, m0m, xs2, m1pb, m1ma, xs1, xs3, t2p, t2m, m1pa, m1mb, m2p, m2m, t1, t3, xs0, xfa, xfb]

    def layer_two(hid, proj, sums2, acc):
        sums2[PAIRS] = jnp.zeros((TILE, 2 * TILE), BF)

        def columns(s):
            places = (((0, 2), (1, 2)), ((1, 1), (1, 3)), ((0, 1), (0, 3)), ((0, 0), (1, 0)))[s]
            return jnp.concatenate([w2c[ba_of(dx, dz)] for dx, dz in places], axis=1)

        def project(rows, s):
            return jnp.dot(rows, columns(s), preferred_element_type=F32).astype(BF)

        def project_all(s):
            def body(i):
                rows = hid[pl.ds(4 * i, 4)].reshape(16 * TILE, 1024)
                value = project(rows, s).reshape(16, TILE, 2 * TILE)
                proj[pl.ds(16 * i, 16), :, pl.ds(s % 2 * 2 * TILE, 2 * TILE)] = value

            each(NA // 4, body)

        def hidden_of(one, two):
            rows = [lows[pl.ds(o * 4, 4)].reshape(4 * TILE, TILE) for o in (one, two)]
            value = jnp.dot(jnp.concatenate(rows, axis=0), w1_ref[...], preferred_element_type=F32) + b1_ref[...]
            value = jnp.maximum(value, 0.0).astype(BF)
            hid[one] = value[: 4 * TILE]
            hid[two] = value[4 * TILE :]
            value = project(value, 0).reshape(8, TILE, 2 * TILE)
            proj[pl.ds(one * 4, 4), :, pl.ds(0, 2 * TILE)] = value[:4]
            proj[pl.ds(two * 4, 4), :, pl.ds(0, 2 * TILE)] = value[4:]

        finish_d = gather(lows, ds_sem, dr_sem, gs_sem, gr_sem, hidden_of)
        finish_d()

        def store2(q, value):
            sums2[q] = value.astype(BF)

        def pick(r):
            value = sums2[index[2, r]].astype(F32)
            return value[:, :TILE], value[:, TILE:]

        def got(i):
            return rb[i].astype(F32)

        def put(i, value):
            sb[i] = value.astype(BF)

        pair_products(proj, 0 * TILE, 2 * TILE, acc, store2)

        def body(i):
            near, far = pick(i)
            put(M0P + i, near)
            put(M0P + H1 + i, far)
            near, far = pick(H1 + i)
            put(M0M + i, near)
            put(M0M + H1 + i, far)

        each(H1, body)
        m0p.start()
        m0m.start()

        def body(i):
            near, far = pick(N1 + i)
            put(T2 + i, near)
            put(XS + 2 * N2 + i, far)

        each(N2, body)
        xs2.start()

        project_all(1)

        pair_products(proj, 2 * TILE, 2 * TILE, acc, store2)

        def body(i):
            plus, minus = pick(N1 + i)
            put(XS + N2 + i, plus)
            put(XS + 3 * N2 + i, minus)

        each(N2, body)
        xs1.start()
        xs3.start()

        def body(i):
            put(M1M + i, pick(i)[1])
            put(M1P + H1 + i, pick(H1 + i)[0])

        each(H1, body)
        m1pb.start()
        m1ma.start()

        project_all(2)
        m0p.wait_recv()
        m0m.wait_recv()

        def body(i):
            put(M1P + i, pick(i)[0] + got(M0P + H1 + i))
            put(M1M + H1 + i, pick(H1 + i)[1] + got(M0M + H1 + i))

        each(H1, body)
        m1pa.start()
        m1mb.start()
        xs2.wait_recv()

        def body(i):
            put(T2 + i, sb[T2 + i].astype(F32) + got(XS + 2 * N2 + i))

        each(N2, body)
        t2p.start()
        t2m.start()

        pair_products(proj, 0 * TILE, 2 * TILE, acc, store2)

        def body(i):
            plus, minus = pick(i)
            put(M2P + i, plus + got(M0P + i))
            put(M2M + i, minus)
            plus, minus = pick(H1 + i)
            put(M2P + H1 + i, plus)
            put(M2M + H1 + i, minus + got(M0M + i))

        each(H1, body)
        m2p.start()
        m2m.start()

        def body(i):
            plus, minus = pick(N1 + i)
            put(T1 + i, plus)
            put(T3 + i, minus)

        each(N2, body)
        project_all(3)

        pair_products(proj, 2 * TILE, 2 * TILE, acc, store2)

        def body(i):
            put(XS + i, pick(N1 + i)[1])

        each(N2, body)
        xs0.start()
        m1pb.wait_recv()
        m1ma.wait_recv()
        m1pa.wait_recv()
        m1mb.wait_recv()

        def body(i):
            put(XF + i, pick(i)[1] + got(M1P + i) + got(M1M + i))

        each(X1, body)
        xfa.start()

        def body(i):
            j = X1 + i
            put(XF + j, pick(j)[1] + got(M1P + j) + got(M1M + j))

        each(N1 - X1, body)
        xfb.start()

        for copy in (xs1, xs3, t2p, t2m):
            copy.wait_recv()

        def body(i):
            j = H2 + i
            put(T1 + i, sb[T1 + i].astype(F32) + got(XS + N2 + i) + got(T2 + i))
            put(T1 + j, sb[T1 + j].astype(F32) + got(XS + N2 + j))
            put(T3 + i, sb[T3 + i].astype(F32) + got(XS + 3 * N2 + i))
            put(T3 + j, sb[T3 + j].astype(F32) + got(XS + 3 * N2 + j) + got(T2 + j))

        each(H2, body)
        t1.start()
        t3.start()

        def write(r, value):
            out_ref[r] = value.astype(BF)

        def flush(i, start, count):
            return pltpu.make_async_copy(out_ref.at[pl.ds(start, count)], out_hbm.at[pl.ds(start, count)], loc_sem.at[16 + i])

        flushes = [flush(0, N1, N2), flush(1, 0, X1), flush(2, X1, N1 - X1)]

        def rows_of(start, count, copy, copy_out):
            copy.wait_recv()

            def body(i):
                j = start + i
                write(j, pick(j)[0] + got(M2P + j) + got(M2M + j) + got(XF + j))

            each(count, body)
            copy_out.start()

        m2p.wait_recv()
        m2m.wait_recv()
        rows_of(0, X1, xfa, flushes[1])
        xs0.wait_recv()
        t1.wait_recv()
        t3.wait_recv()

        def body(i):
            write(N1 + i, pick(N1 + i)[0] + got(XS + i) + got(T1 + i) + got(T3 + i))

        each(N2, body)
        flushes[0].start()
        rows_of(X1, N1 - X1, xfb, flushes[2])
        for copy in messages:
            copy.wait_send()
        for copy_out in flushes:
            copy_out.wait()

    for copy in w2_copies + late:
        copy.wait()
    pl.run_scoped(
        layer_two,
        pltpu.VMEM((NA, 4 * TILE, 1024), BF),
        pltpu.VMEM((64, TILE, 4 * TILE), BF),
        pltpu.VMEM((PAIRS + 1, TILE, 2 * TILE), BF),
        pltpu.VMEM((TILE, 2 * TILE), F32),
    )


def on_device(features, tile_values, tile_row, tile_col, weight_one, bias_one, weight_two):
    hbm = pl.BlockSpec(memory_space=pl.ANY)
    dma = pltpu.SemaphoreType.DMA
    return pl.pallas_call(
        kernel,
        out_shape=jax.ShapeDtypeStruct((RB, TILE, TILE), BF),
        in_specs=[hbm] * 7,
        out_specs=hbm,
        scratch_shapes=[
            pltpu.VMEM((129, TILE, TILE), BF),
            pltpu.VMEM((NB, 1024, TILE), BF),
            pltpu.VMEM((64, TILE, TILE), BF),
            pltpu.VMEM((C_BLOCKS, TILE, TILE), F32),
            pltpu.VMEM((64, TILE, TILE), BF),
            pltpu.VMEM((BLOCKS, TILE, TILE), BF),
            pltpu.VMEM((BLOCKS, TILE, TILE), BF),
            pltpu.VMEM((8, 2 * TILE), jnp.int32),
            pltpu.VMEM((8, TILE), F32),
            pltpu.SMEM((8, 2 * TILE), jnp.int32),
            pltpu.SMEM((8, TILE), F32),
            pltpu.VMEM((1, TILE), jnp.int32),
            pltpu.VMEM((1, TILE), jnp.int32),
            pltpu.VMEM((TILE, 1024), BF),
            pltpu.VMEM((1, 1024), F32),
            pltpu.VMEM((RB, TILE, TILE), BF),
        ]
        + [dma((19,))]
        + [dma((12,))] * 4
        + [dma((15,))] * 2
        + [dma((12,))] * 4
        + [dma((18,))] * 2,
        compiler_params=pltpu.CompilerParams(
            collective_id=0, has_side_effects=True, vmem_limit_bytes=64 * 2**20 - 2**16
        ),
        cost_estimate=pl.CostEstimate(flops=26 * 10**9, bytes_accessed=8 * 2**20, transcendentals=0),
        name="two_layers",
    )(tile_row.reshape(1, -1), tile_col.reshape(1, -1), features.reshape(4, TILE, TILE), tile_values, weight_one, bias_one.reshape(1, -1), weight_two).reshape(RB * TILE, TILE)


def solution(mesh):
    return jax.shard_map(
        on_device,
        mesh=mesh,
        in_specs=(
            P(("aa", "ba"), None),
            P(("aa", "ba"), None, None),
            P(("aa", "ba")),
            P(("aa", "ba")),
            P(),
            P(),
            P(),
        ),
        out_specs=P("aa", "ba"),
        check_vma=False,
    )
```
